32 devices in a mesh: orbit: 8 (over z, y), space: 4 (over x, core).
Axes of the slice: x: 2, y: 2, z: 4, core: 2. Of those that a mesh axis runs over, the one named last changes fastest.
Arguments:
- latents: bfloat16 [32, 4, 16, 1024], P('orbit', 'space'), may hold values from -6 to 6
- conv_gain: float32 [1024], replicated, may hold values from 0.1 to 1.9
- spatial_weight: bfloat16 [3, 3, 1024, 1024], P(None, None, 'space'), may hold values from -0.0625 to 0.0625
- temporal_weight: bfloat16 [3, 1024, 1024], P(None, 'space'), may hold values from -0.109375 to 0.109375
- attn_gain: float32 [1024], replicated, may hold values from 0.1 to 1.9
- qkv_weight: bfloat16 [3, 1024, 1024], P(None, 'space'), may hold values from -0.1875 to 0.1875
- out_weight: bfloat16 [1024, 1024], P('space'), may hold values from -0.1875 to 0.1875
Outputs:
- restored: bfloat16 [32, 4, 16, 1024], P('orbit', 'space')
The draws below stay inside these ranges and needn't reach their ends.
All inputs are finite; a program needn't handle non-finite values.
Results may differ from the reference program's by a relative error of at most 0.029.
Values may be sent and summed in bfloat16 or wider, within the bound.
No kernel may reach another device: no remote copies, remote signals or barrier semaphores. Data moves between devices by JAX's collectives and lax.ppermute only.
A program may use at most 64 MiB of HBM per device.

```python
import jax
import jax.numpy as jnp
from jax import lax

C = 1024
HEADS = 16
HD = 64
W = 16
F = 32
H = 4


def levels(own_key, extent, pieces, low, high):
    level, own = 1.0, jax.random.fold_in(own_key, 6)
    for position, shards_of in pieces:
        steps = jnp.exp(jax.random.uniform(jax.random.fold_in(own, position), (shards_of,), jnp.float32, low / len(pieces), high / len(pieces)))
        level = level * jnp.repeat(steps, extent[position] // shards_of).reshape([-1 if axis == position else 1 for axis in range(len(extent))])
    return level


def gaussian(rng, shape, spread, bound, split=(), held_as=jnp.bfloat16):
    values = jax.random.normal(rng, shape, jnp.float32) * spread
    if len(split) > 0:
        values = levels(rng, shape, split, -0.22, 0.18) * values
    return jnp.clip(values, min=-bound, max=bound).astype(held_as)


def setup_inputs(seed: int = 0) -> dict:
    splits = jax.random.split(jax.random.key(seed), 8)
    latents = gaussian(splits[0], (F, H, W, C), 1.0, 6.0, ((0, 8), (1, 4)))
    conv_gain = jnp.clip(1.0 + 0.18 * jax.random.normal(splits[1], (C,), jnp.float32), 0.1, 1.9)
    spatial_weight = gaussian(splits[2], (3, 3, C, C), (9 * C) ** -0.5, 0.0625, ((2, 4),))
    temporal_weight = gaussian(splits[3], (3, C, C), (3 * C) ** -0.5, 0.109375, ((1, 4),))
    attn_gain = jnp.clip(1.0 + 0.18 * jax.random.normal(splits[4], (C,), jnp.float32), 0.1, 1.9)
    qkv_weight = gaussian(splits[5], (3, C, C), C ** -0.5, 0.1875, ((1, 4),))
    out_weight = gaussian(splits[6], (C, C), C ** -0.5, 0.1875, ((0, 4),))
    return {"latents": latents, "conv_gain": conv_gain, "spatial_weight": spatial_weight, "temporal_weight": temporal_weight, "attn_gain": attn_gain, "qkv_weight": qkv_weight, "out_weight": out_weight}


def rms_scale(values, gain):
    wide = values.astype(jnp.float32)
    return wide * lax.rsqrt(lax.optimization_barrier(jnp.mean(wide * wide, axis=-1, keepdims=True)) + 1e-06) * gain

def dot_trans(left, right):
    return lax.dot_general(left, right, (((1,), (1,)), ((), ())), preferred_element_type=jnp.float32)

def reference(latents, conv_gain, spatial_weight, temporal_weight, attn_gain, qkv_weight, out_weight):
    frames, rows, cols, chans = latents.shape
    normed = rms_scale(latents, conv_gain).astype(jnp.bfloat16)
    padded = jnp.pad(normed, ((0, 0), (1, 1), (1, 1), (0, 0)))
    total = jnp.zeros((frames * rows * cols, chans), jnp.float32)
    for i in range(3):
        for j in range(3):
            window = padded[:, i:i + rows, j:j + cols, :].reshape(-1, chans)
            total = total + dot_trans(window, spatial_weight[i, j])
    activated = jax.nn.silu(total).astype(jnp.bfloat16).reshape(frames, rows, cols, chans)
    before = jnp.roll(activated, 1, axis=0)[0::2].reshape(-1, chans)
    even = activated[0::2].reshape(-1, chans)
    odd = activated[1::2].reshape(-1, chans)
    down32 = jnp.dot(before, temporal_weight[0], preferred_element_type=jnp.float32)
    down32 = down32 + jnp.dot(even, temporal_weight[1], preferred_element_type=jnp.float32)
    down32 = down32 + jnp.dot(odd, temporal_weight[2], preferred_element_type=jnp.float32)
    down = down32.astype(jnp.bfloat16)
    down_normed = rms_scale(down, attn_gain).astype(jnp.bfloat16)
    half = frames // 2
    shape5 = (half, rows, cols, HEADS, HD)
    query = dot_trans(down_normed, qkv_weight[0]).astype(jnp.bfloat16).reshape(shape5)
    key = dot_trans(down_normed, qkv_weight[1]).astype(jnp.bfloat16).reshape(shape5)
    value = dot_trans(down_normed, qkv_weight[2]).astype(jnp.bfloat16).reshape(shape5)
    scores = jnp.einsum('thwnd,shwnd->hwnts', query.astype(jnp.float32), key.astype(jnp.float32)) / jnp.sqrt(jnp.float32(HD))
    probs = jax.nn.softmax(scores, axis=-1).astype(jnp.bfloat16)
    mixed = jnp.einsum('hwnts,shwnd->thwnd', probs.astype(jnp.float32), value.astype(jnp.float32)).astype(jnp.bfloat16)
    projected = jnp.dot(mixed.reshape(-1, chans), out_weight, preferred_element_type=jnp.float32)
    bottom = (down.astype(jnp.float32) + projected).astype(jnp.bfloat16).reshape(half, rows, cols, chans)
    grown = jnp.repeat(bottom, 2, axis=0)
    return (latents.astype(jnp.float32) + grown.astype(jnp.float32)).astype(jnp.bfloat16)
```

```python
import functools

import jax
import jax.numpy as jnp
from jax import lax
from jax.experimental import pallas as pl
from jax.experimental.pallas import tpu as pltpu
from jax.sharding import PartitionSpec as P

HD = 64
CORES = 2
F32 = jnp.float32
BF16 = jnp.bfloat16


def dot(left, right):
    return jnp.dot(left, right, preferred_element_type=F32)


def dot_trans(left, right):
    return lax.dot_general(left, right, (((1,), (1,)), ((), ())), preferred_element_type=F32)


def rms_scale(wide, gain):
    return wide * lax.rsqrt(jnp.mean(wide * wide, axis=-1, keepdims=True) + 1e-06) * gain


def split_by(number, size):
    if size & (size - 1) == 0:
        quotient = number >> (size.bit_length() - 1)
    else:
        quotient = (number * (65536 // size + 1)) >> 16
    return quotient, number - quotient * size


def digits(count, sizes):
    number = lax.broadcasted_iota(jnp.int32, (count, 1), 0)
    found = []
    for size in reversed(sizes[1:]):
        number, digit = split_by(number, size)
        found.append(digit)
    return [number] + found[::-1]


def picks(source, width):
    columns = lax.broadcasted_iota(jnp.int32, (source.shape[0], width), 1)
    return columns == source


def as_weights(mask):
    return jnp.where(mask, 1.0, 0.0).astype(BF16)


class Plan:
    def __init__(self, orbit, space, cols, chans, slice_chans):
        self.orbit, self.space, self.cols, self.chans = orbit, space, cols, chans
        self.slice_chans = slice_chans
        self.x = space // CORES
        self.ncol = cols // orbit
        self.peers = orbit * self.x
        self.pixels = self.x * self.ncol
        self.views = 2 * orbit
        self.half_rows = self.views * self.pixels
        sets = 3 * self.pixels
        self.in_lanes = next(n for n in (1, 2, 4, 8) if sets * n % 8 == 0)
        self.in_rows, self.in_width = sets * self.in_lanes, chans // self.in_lanes
        back = 2 * self.ncol
        self.out_lanes = next(n for n in (1, 2, 4, 8) if back * n % 8 == 0)
        self.out_rows, self.out_width = back * self.out_lanes, chans // self.out_lanes


def conv_kernel(plan, x_ref, gain_ref, weight_ref, temporal_ref, send_ref, keep_ref, normed):
    rows, per_row = x_ref.shape[0], x_ref.shape[1]
    cols, depth = plan.cols, plan.slice_chans
    gain = gain_ref[...]
    for r in range(rows):
        normed[r * per_row : (r + 1) * per_row] = rms_scale(x_ref[r].astype(F32), gain).astype(BF16)
    count = rows * per_row
    column = split_by(lax.broadcasted_iota(jnp.int32, (count, 1), 0), cols)[1]
    total = None
    for j in (1, 0, 2):
        part = dot_trans(normed[...], weight_ref[1, j])
        above = dot_trans(normed[: count - per_row], weight_ref[0, j])
        below = dot_trans(normed[per_row:], weight_ref[2, j])
        edge = jnp.zeros((per_row, depth), F32)
        part = part + jnp.concatenate([edge, above]) + jnp.concatenate([below, edge])
        if j == 0:
            part = jnp.where(column == 0, 0.0, pltpu.roll(part, 1, 0))
        if j == 2:
            part = jnp.where(column == cols - 1, 0.0, pltpu.roll(part, count - 1, 0))
        total = part if total is None else total + part
    activated = (total / (1.0 + jnp.exp(-total))).astype(BF16)
    activated = activated.reshape(rows, per_row // cols, cols, depth)
    pixels = rows * cols
    even = [activated[:, f].reshape(pixels, depth) for f in (0, 2)]
    odd = [activated[:, f].reshape(pixels, depth) for f in (1, 3)]
    even, odd = jnp.concatenate(even), jnp.concatenate(odd)
    first, second, third = dot(odd, temporal_ref[0]), dot(even, temporal_ref[1]), dot(odd, temporal_ref[2])
    own = second + third
    sets = jnp.concatenate([own[:pixels], own[pixels:] + first[:pixels], first[pixels:]]).astype(BF16)
    width = plan.in_width
    stacked = jnp.concatenate([sets[:, k * width : (k + 1) * width] for k in range(plan.in_lanes)])
    core = lax.rem(lax.axis_index("space"), CORES)
    count = plan.orbit * plan.in_rows
    o, lane, which, r, c = digits(count, (plan.orbit, plan.in_lanes, 3, plan.x, plan.ncol))
    source = lane * (3 * pixels) + which * pixels + r * (CORES * cols) + o * plan.ncol + c
    for ref, parity in ((send_ref, 1 - core), (keep_ref, core)):
        ref[...] = dot(as_weights(picks(source + parity * cols, stacked.shape[0])), stacked).astype(BF16)


def norm_kernel(plan, got_ref, gain_ref, down_ref, normed_ref):
    o, t, r, c = digits(plan.half_rows, (plan.orbit, 2, plan.x, plan.ncol))
    width = plan.peers * plan.in_rows
    peer, lane, which, pixel = None, None, None, None
    number = lax.broadcasted_iota(jnp.int32, (1, width), 1)
    number, pixel = split_by(number, plan.pixels)
    number, which = split_by(number, 3)
    number, lane = split_by(number, plan.in_lanes)
    sender, _ = split_by(number, plan.x)
    before = jnp.where(o == 0, plan.orbit - 1, o - 1)
    same = (which == t) & (sender == o)
    edge = (which == 2) & (sender == before) & (t == 0)
    wanted = (pixel == r * plan.ncol + c) & (same | edge)
    got = got_ref[...]
    down = [dot(as_weights(wanted & (lane == k)), got) for k in range(plan.in_lanes)]
    down = jnp.concatenate(down, axis=1).astype(BF16)
    down_ref[...] = down
    normed_ref[...] = rms_scale(down.astype(F32), gain_ref[...]).astype(BF16)


def attend_kernel(plan, own_ref, other_ref, down_ref, qkv_ref, out_ref, send_ref, keep_ref):
    half, depth = plan.half_rows, plan.slice_chans
    heads = depth // HD
    flat = jnp.concatenate([own_ref[...], other_ref[...]])
    query, key, value = [dot_trans(flat, qkv_ref[k]).astype(BF16) for k in range(3)]
    lane_head = lax.broadcasted_iota(jnp.int32, (1, depth), 1) >> (HD.bit_length() - 1)
    count = 2 * half
    wide = query.astype(F32)
    query = jnp.concatenate([jnp.where(lane_head == h, wide, 0.0) for h in range(heads)]).astype(BF16)
    scores = dot_trans(query, key) * (HD**-0.5)
    row = lax.broadcasted_iota(jnp.int32, (heads * count, 1), 0) & (count - 1)
    column = lax.broadcasted_iota(jnp.int32, (1, count), 1)
    low, shift = plan.pixels - 1, half.bit_length() - 1
    same = ((row & low) == (column & low)) & ((row >> shift) == (column >> shift))
    top = jnp.max(jnp.where(same, scores, -jnp.inf), axis=-1, keepdims=True)
    weights = jnp.where(same, jnp.exp(scores - top), 0.0)
    probs = (weights / jnp.sum(weights, axis=-1, keepdims=True)).astype(BF16)
    found = dot(probs, value)
    mixed = jnp.zeros((count, depth), F32)
    for h in range(heads):
        mixed = jnp.where(lane_head == h, found[h * count : (h + 1) * count], mixed)
    projected = dot(mixed.astype(BF16), out_ref[...])
    first = lax.axis_index("space") < CORES
    kept = projected[:half] + jnp.where(first, 1.0, 0.0) * down_ref[...].astype(F32)
    rows = plan.peers * plan.out_rows
    o, r, lane, t, c = digits(rows, (plan.orbit, plan.x, plan.out_lanes, 2, plan.ncol))
    source = lane * half + ((o * 2 + t) * plan.x + r) * plan.ncol + c
    order = as_weights(picks(source, plan.out_lanes * half))
    width = plan.out_width
    for ref, block in ((send_ref, projected[half:]), (keep_ref, kept)):
        block = block.astype(BF16)
        block = jnp.concatenate([block[:, k * width : (k + 1) * width] for k in range(plan.out_lanes)])
        ref[...] = dot(order, block).astype(BF16)


def end_kernel(plan, got_ref, latents_ref, out_ref):
    rows = 2 * plan.cols
    t, o, c = digits(rows, (2, plan.orbit, plan.ncol))
    number = lax.broadcasted_iota(jnp.int32, (1, got_ref.shape[0]), 1)
    number, column = split_by(number, plan.ncol)
    number, view = split_by(number, 2)
    number, lane = split_by(number, plan.out_lanes)
    sender, _ = split_by(number, plan.x)
    wanted = (sender == o) & (column == c) & (view == t)
    got = got_ref[...]
    bottom = [dot(as_weights(wanted & (lane == k)), got) for k in range(plan.out_lanes)]
    bottom = jnp.concatenate(bottom, axis=1).astype(BF16).astype(F32)
    for f in range(4):
        block = bottom[(f // 2) * plan.cols : (f // 2 + 1) * plan.cols]
        out_ref[f] = (latents_ref[f].astype(F32) + block).astype(BF16)


def call(kernel, name, shapes, args, scratch=(), flops=0):
    whole = pl.BlockSpec(memory_space=pltpu.VMEM)
    outs = [jax.ShapeDtypeStruct(shape, BF16) for shape in shapes]
    moved = sum(a.size * a.dtype.itemsize for a in (*args, *outs))
    return pl.pallas_call(
        kernel,
        out_shape=outs,
        in_specs=[whole] * len(args),
        out_specs=[whole] * len(outs),
        scratch_shapes=list(scratch),
        compiler_params=pltpu.CompilerParams(vmem_limit_bytes=40 * 2**20),
        cost_estimate=pl.CostEstimate(flops=flops, bytes_accessed=moved, transcendentals=0),
        name=name,
    )(*args)


def body(latents, conv_gain, spatial_weight, temporal_weight, attn_gain, qkv_weight, out_weight):
    views, _, cols, chans = latents.shape
    orbit, space = lax.axis_size("orbit"), lax.axis_size("space")
    plan = Plan(orbit, space, cols, chans, spatial_weight.shape[2])
    both = ("orbit", "space")
    groups = [
        [(o * plan.x + x) * CORES + core for o in range(orbit) for x in range(plan.x)]
        for core in range(CORES)
    ]
    chip = [(s, s ^ 1) for s in range(space)]

    own = latents.reshape(views * cols, chans)
    gathered = lax.all_gather(own, "space", axis=0)
    shape = (orbit * plan.in_rows, plan.in_width)
    send, keep = call(
        functools.partial(conv_kernel, plan),
        "conv",
        [shape, shape],
        (gathered, conv_gain.reshape(1, chans), spatial_weight, temporal_weight),
        [pltpu.VMEM((space * views * cols, chans), BF16)],
        flops=2 * 9 * space * views * cols * chans * plan.slice_chans,
    )
    partial_sum = keep.astype(F32) + lax.ppermute(send, "space", chip).astype(F32)
    partial_sum = partial_sum.astype(BF16).reshape(orbit, 1, plan.in_rows, plan.in_width)
    spread = jnp.broadcast_to(partial_sum, (orbit, plan.x, plan.in_rows, plan.in_width))
    spread = spread.reshape(plan.peers, plan.in_rows, plan.in_width)
    got = lax.all_to_all(spread, both, 0, 0, tiled=True, axis_index_groups=groups)
    shape = (plan.half_rows, chans)
    down, normed = call(
        functools.partial(norm_kernel, plan),
        "down_norm",
        [shape, shape],
        (got.reshape(plan.peers * plan.in_rows, plan.in_width), attn_gain.reshape(1, chans)),
    )
    other = lax.ppermute(normed, "space", chip)
    shape = (plan.peers * plan.out_rows, plan.out_width)
    send, keep = call(
        functools.partial(attend_kernel, plan),
        "attend",
        [shape, shape],
        (normed, other, down, qkv_weight, out_weight),
        flops=2 * 4 * 2 * plan.half_rows * chans * plan.slice_chans,
    )
    partial_sum = keep.astype(F32) + lax.ppermute(send, "space", chip).astype(F32)
    partial_sum = partial_sum.astype(BF16).reshape(plan.peers, plan.out_rows, plan.out_width)
    got = lax.all_to_all(partial_sum, both, 0, 0, tiled=True, axis_index_groups=groups)
    (restored,) = call(
        functools.partial(end_kernel, plan),
        "restore",
        [(views, cols, chans)],
        (got.reshape(shape), latents.reshape(views, cols, chans)),
    )
    return restored.reshape(latents.shape)


def solution(mesh):
    return jax.shard_map(
        body,
        mesh=mesh,
        in_specs=(
            P("orbit", "space", None, None),
            P(),
            P(None, None, "space", None),
            P(None, "space", None),
            P(),
            P(None, "space", None),
            P("space", None),
        ),
        out_specs=P("orbit", "space", None, None),
        check_vma=False,
    )
```

```python
import functools

import jax
import jax.numpy as jnp
import numpy as np
from jax import lax
from jax.experimental import pallas as pl
from jax.experimental.pallas import tpu as pltpu
from jax.sharding import PartitionSpec as P

HD = 64
CORES = 2
F32 = jnp.float32
BF16 = jnp.bfloat16


def dot(left, right):
    return jnp.dot(left, right, preferred_element_type=F32)


def dot_trans(left, right):
    return lax.dot_general(left, right, (((1,), (1,)), ((), ())), preferred_element_type=F32)


def rms_scale(wide, gain):
    return wide * lax.rsqrt(jnp.mean(wide * wide, axis=-1, keepdims=True) + 1e-06) * gain


def picks(source, width):
    return jnp.asarray(np.asarray(source).reshape(-1, 1) == np.arange(width), BF16)


class Plan:
    def __init__(self, orbit, space, views, cols, chans, slice_chans):
        self.orbit, self.space, self.views = orbit, space, views
        self.cols, self.chans, self.slice_chans = cols, chans, slice_chans
        self.x = space // CORES
        self.ncol = cols // orbit
        self.pixels = self.x * self.ncol
        self.down_views = views // 2 * orbit
        self.down_rows = self.down_views * self.pixels
        self.send_rows = views * self.pixels
        back = views // 2 * self.ncol
        self.lanes = next(n for n in (1, 2, 4, 8) if back * n % 8 == 0)
        self.back_rows, self.back_width = back * self.lanes, chans // self.lanes

    def send_order(self):
        o, core, odd, pair, r, c = np.indices((self.orbit, CORES, 2, self.views // 2, self.x, self.ncol))
        row, view, col = r * CORES + core, 2 * pair + odd, o * self.ncol + c
        return picks((row * self.views + view) * self.cols + col, self.space * self.views * self.cols)

    def back_order(self):
        o, r, lane, t, c = np.indices((self.orbit, self.x, self.lanes, self.views // 2, self.ncol))
        view = o * (self.views // 2) + t
        source = lane * self.down_rows + (view * self.x + r) * self.ncol + c
        return picks(source, self.lanes * self.down_rows)

    def end_order(self):
        sender, _, lane, view, c = np.indices((self.orbit, self.x, self.lanes, self.views // 2, self.ncol))
        target = view * self.cols + sender * self.ncol + c
        parts = []
        for k in range(self.lanes):
            wanted = np.where(lane == k, target, -1).reshape(1, -1)
            parts.append(wanted == np.arange(self.views // 2 * self.cols).reshape(-1, 1))
        return jnp.asarray(np.stack(parts), BF16)


def norm_kernel(gain_ref, *refs):
    count = len(refs) // 2
    for x_ref, out_ref in zip(refs[:count], refs[count:]):
        out_ref[...] = rms_scale(x_ref[...].astype(F32), gain_ref[...]).astype(BF16)


def conv_kernel(plan, gain_ref, weight_ref, order_ref, *refs):
    x_refs, (out_ref, normed) = refs[:-2], refs[-2:]
    per_row, cols, depth = plan.views * plan.cols, plan.cols, plan.slice_chans
    gain = gain_ref[...]
    space = lax.axis_index("space")
    ready = plan.x + 1
    for k, x_ref in enumerate(x_refs):
        block = x_ref[...]
        if k >= ready:
            block = rms_scale(block.astype(F32), gain).astype(BF16)
        index = k if k < 2 else (k - 1) * CORES if k < ready else (k - ready + 1) * CORES + 1
        normed[space ^ index] = block
    count = plan.space * per_row
    rows = normed[...].reshape(count, plan.chans)
    column = lax.broadcasted_iota(jnp.int32, (count, 1), 0) & (cols - 1)
    total = None
    for j in (1, 0, 2):
        part = dot_trans(rows, weight_ref[1, j])
        above = dot_trans(rows[: count - per_row], weight_ref[0, j])
        below = dot_trans(rows[per_row:], weight_ref[2, j])
        edge = jnp.zeros((per_row, depth), F32)
        part = part + jnp.concatenate([edge, above]) + jnp.concatenate([below, edge])
        if j == 0:
            part = jnp.where(column == 0, 0.0, pltpu.roll(part, 1, 0))
        if j == 2:
            part = jnp.where(column == cols - 1, 0.0, pltpu.roll(part, count - 1, 0))
        total = part if total is None else total + part
    activated = (total / (1.0 + jnp.exp(-total))).astype(BF16)
    out_ref[...] = dot(order_ref[...], activated).astype(BF16)


def temporal_kernel(plan, got_ref, own_ref, other_ref, out_ref):
    core = lax.rem(lax.axis_index("space"), CORES)
    half, depth = plan.send_rows // 2, plan.slice_chans
    total = None
    for index, weight_ref in ((core, own_ref), (1 - core, other_ref)):
        block = got_ref[:, index].astype(F32)
        even = block[:, :half].reshape(plan.down_rows, depth)
        odd = block[:, half:].reshape(plan.down_rows, depth)
        before = pltpu.roll(odd, plan.pixels, 0)
        for k, rows in enumerate((before, even, odd)):
            part = dot(rows.astype(BF16), weight_ref[k])
            total = part if total is None else total + part
    out_ref[...] = total.astype(BF16)


def attend_kernel(plan, gain_ref, order_ref, own_qkv, other_qkv, own_out, other_out, *refs):
    down_refs, out_ref = refs[:-1], refs[-1]
    rows, depth = plan.down_rows, plan.slice_chans
    heads = depth // HD
    down = down_refs[0][...].astype(F32)
    for ref in down_refs[1:]:
        down = down + ref[...].astype(F32)
    down = down.astype(BF16).astype(F32)
    normed = rms_scale(down, gain_ref[...]).astype(BF16)
    lane_head = lax.broadcasted_iota(jnp.int32, (1, depth), 1) >> (HD.bit_length() - 1)
    low = plan.pixels - 1
    row = lax.broadcasted_iota(jnp.int32, (heads * rows, 1), 0) & low
    column = lax.broadcasted_iota(jnp.int32, (1, rows), 1) & low
    same = row == column
    first = lax.axis_index("space") < CORES
    projected = jnp.where(first, 1.0, 0.0) * down
    for qkv_ref, weight_ref in ((own_qkv, own_out), (other_qkv, other_out)):
        query, key, value = [dot_trans(normed, qkv_ref[k]).astype(BF16) for k in range(3)]
        wide = query.astype(F32)
        query = jnp.concatenate([jnp.where(lane_head == h, wide, 0.0) for h in range(heads)]).astype(BF16)
        scores = dot_trans(query, key) * (HD**-0.5)
        top = jnp.max(jnp.where(same, scores, -jnp.inf), axis=-1, keepdims=True)
        weights = jnp.where(same, jnp.exp(scores - top), 0.0)
        probs = (weights / jnp.sum(weights, axis=-1, keepdims=True)).astype(BF16)
        found = dot(probs, value)
        mixed = found[:rows]
        for h in range(1, heads):
            mixed = jnp.where(lane_head == h, found[h * rows : (h + 1) * rows], mixed)
        projected = projected + dot(mixed.astype(BF16), weight_ref[...])
    projected = projected.astype(BF16)
    width = plan.back_width
    stacked = jnp.concatenate([projected[:, k * width : (k + 1) * width] for k in range(plan.lanes)])
    out_ref[...] = dot(order_ref[...], stacked).astype(BF16)


def end_kernel(plan, got_ref, order_ref, latents_ref, out_ref):
    got = got_ref[...]
    bottom = [dot(order_ref[k], got) for k in range(plan.lanes)]
    bottom = jnp.concatenate(bottom, axis=1).astype(BF16).astype(F32)
    for f in range(plan.views):
        block = bottom[(f // 2) * plan.cols : (f // 2 + 1) * plan.cols]
        out_ref[f] = (latents_ref[f].astype(F32) + block).astype(BF16)


def call(kernel, name, shapes, args, scratch=(), flops=0, space=pltpu.VMEM):
    outs = [s if isinstance(s, jax.ShapeDtypeStruct) else jax.ShapeDtypeStruct(s, BF16) for s in shapes]
    moved = sum(a.size * a.dtype.itemsize for a in (*args, *outs))
    return pl.pallas_call(
        kernel,
        out_shape=outs,
        in_specs=[pl.BlockSpec(memory_space=space)] * len(args),
        out_specs=[pl.BlockSpec(memory_space=pltpu.VMEM)] * len(outs),
        scratch_shapes=list(scratch),
        compiler_params=pltpu.CompilerParams(vmem_limit_bytes=40 * 2**20),
        cost_estimate=pl.CostEstimate(flops=flops, bytes_accessed=moved, transcendentals=0),
        name=name,
    )(*args)


def body(latents, conv_gain, spatial_weight, temporal_weight, attn_gain, qkv_weight, out_weight):
    views, _, cols, chans = latents.shape
    orbit, space = lax.axis_size("orbit"), lax.axis_size("space")
    plan = Plan(orbit, space, views, cols, chans, spatial_weight.shape[2])
    conv_gain, attn_gain = conv_gain.reshape(1, chans), attn_gain.reshape(1, chans)

    def swap(block, distance):
        return lax.ppermute(block, "space", [(s, s ^ distance) for s in range(space)])

    def exchange(blocks, groups):
        return lax.all_to_all(blocks, ("orbit", "space"), 0, 0, tiled=True, axis_index_groups=groups)

    by_core = [[o * space + x * CORES + c for o in range(orbit) for c in range(CORES)] for x in range(plan.x)]
    by_x = [[o * space + x * CORES + c for o in range(orbit) for x in range(plan.x)] for c in range(CORES)]

    own = latents.reshape(views * cols, chans)
    far = [swap(own, x * CORES) for x in range(1, plan.x)]
    near = swap(own, 1)
    (normed,) = call(norm_kernel, "norm_own", [own.shape], (conv_gain, own), flops=6 * 10**9)
    normed, near, far = lax.optimization_barrier((normed, near, far))
    other_temporal = swap(temporal_weight, 1)
    across = [swap(block, 1) for block in far]
    ready = call(norm_kernel, "norm", [own.shape] * plan.x, (conv_gain, near, *far), flops=6 * 10**9)

    count = space * views * cols
    (activated,) = call(
        functools.partial(conv_kernel, plan),
        "conv",
        [(count, plan.slice_chans)],
        (conv_gain, spatial_weight, plan.send_order(), normed, *ready, *across),
        [pltpu.VMEM((space, views * cols, chans), BF16)],
        flops=2 * 9 * count * chans * plan.slice_chans,
    )
    activated, qkv, out = lax.optimization_barrier((activated, qkv_weight, out_weight))
    other_qkv, other_out = swap(qkv, 1), swap(out, 1)
    got = exchange(activated.reshape(orbit * CORES, plan.send_rows, plan.slice_chans), by_core)
    (down,) = call(
        functools.partial(temporal_kernel, plan),
        "temporal",
        [(plan.down_rows, chans)],
        (got.reshape(orbit, CORES, plan.send_rows, plan.slice_chans), temporal_weight, other_temporal),
        flops=2 * 6 * plan.down_rows * chans * plan.slice_chans,
    )
    downs = [down] + [swap(down, x * CORES) for x in range(1, plan.x)]
    peers = orbit * plan.x
    (back,) = call(
        functools.partial(attend_kernel, plan),
        "attend",
        [(peers * plan.back_rows, plan.back_width)],
        (attn_gain, plan.back_order(), qkv_weight, other_qkv, out_weight, other_out, *downs),
        flops=2 * 8 * plan.down_rows * chans * plan.slice_chans,
    )
    got = exchange(back.reshape(peers, plan.back_rows, plan.back_width), by_x)
    (restored,) = call(
        functools.partial(end_kernel, plan),
        "restore",
        [(views, cols, chans)],
        (got.reshape(peers * plan.back_rows, plan.back_width), plan.end_order(), latents.reshape(views, cols, chans)),
    )
    return restored.reshape(latents.shape)


def solution(mesh):
    return jax.shard_map(
        body,
        mesh=mesh,
        in_specs=(
            P("orbit", "space", None, None),
            P(),
            P(None, None, "space", None),
            P(None, "space", None),
            P(),
            P(None, "space", None),
            P("space", None),
        ),
        out_specs=P("orbit", "space", None, None),
        check_vma=False,
    )
```

```python
import functools

import jax
import jax.numpy as jnp
import numpy as np
from jax import lax
from jax.experimental import pallas as pl
from jax.experimental.pallas import tpu as pltpu
from jax.sharding import PartitionSpec as P

HD = 64
CORES = 2
F32 = jnp.float32
BF16 = jnp.bfloat16


def dot(left, right):
    return jnp.dot(left, right, preferred_element_type=F32)


def dot_trans(left, right):
    return lax.dot_general(left, right, (((1,), (1,)), ((), ())), preferred_element_type=F32)


def rms_scale(wide, gain):
    return wide * lax.rsqrt(jnp.mean(wide * wide, axis=-1, keepdims=True) + 1e-06) * gain


def picks(source, width):
    return jnp.asarray(np.asarray(source).reshape(-1, 1) == np.arange(width), BF16)


class Plan:
    def __init__(self, orbit, space, views, cols, chans, slice_chans):
        self.orbit, self.space, self.views = orbit, space, views
        self.cols, self.chans, self.slice_chans = cols, chans, slice_chans
        self.x = space // CORES
        self.ncol = cols // orbit
        self.pixels = self.x * self.ncol
        self.down_views = views // 2 * orbit
        self.down_rows = self.down_views * self.pixels
        self.send_rows = views * self.pixels
        self.peers = orbit * self.x
        self.back = views // 2 * self.ncol
        self.lanes = next(n for n in (1, 2, 4, 8) if self.back * n % 8 == 0)
        self.back_rows, self.back_width = self.back * self.lanes, chans // self.lanes

    def send_order(self):
        o, core, odd, r, pair, c = np.indices((self.orbit, CORES, 2, self.x, self.views // 2, self.ncol))
        row, view, col = r * CORES + core, 2 * pair + odd, o * self.ncol + c
        return picks((row * self.views + view) * self.cols + col, self.space * self.views * self.cols)

    def end_order(self):
        sender, _, lane, view, c = np.indices((self.orbit, self.x, self.lanes, self.views // 2, self.ncol))
        target = view * self.cols + sender * self.ncol + c
        parts = []
        for k in range(self.lanes):
            wanted = np.where(lane == k, target, -1).reshape(1, -1)
            parts.append(wanted == np.arange(self.views // 2 * self.cols).reshape(-1, 1))
        return jnp.asarray(np.stack(parts), BF16)


def norm_kernel(gain_ref, *refs):
    count = len(refs) // 2
    for x_ref, out_ref in zip(refs[:count], refs[count:]):
        out_ref[...] = rms_scale(x_ref[...].astype(F32), gain_ref[...]).astype(BF16)


def conv_kernel(plan, gain_ref, weight_ref, order_ref, *refs):
    x_refs, (out_ref, normed) = refs[:-2], refs[-2:]
    per_row, cols, depth = plan.views * plan.cols, plan.cols, plan.slice_chans
    gain = gain_ref[...]
    space = lax.axis_index("space")
    ready = plan.x + 1
    for k, x_ref in enumerate(x_refs):
        block = x_ref[...]
        if k >= ready:
            block = rms_scale(block.astype(F32), gain).astype(BF16)
        index = k if k < 2 else (k - 1) * CORES if k < ready else (k - ready + 1) * CORES + 1
        normed[space ^ index] = block
    count = plan.space * per_row
    rows = normed[...].reshape(count, plan.chans)
    column = lax.broadcasted_iota(jnp.int32, (count, 1), 0) & (cols - 1)
    total = None
    for j in (1, 0, 2):
        part = dot_trans(rows, weight_ref[1, j])
        above = dot_trans(rows[: count - per_row], weight_ref[0, j])
        below = dot_trans(rows[per_row:], weight_ref[2, j])
        edge = jnp.zeros((per_row, depth), F32)
        part = part + jnp.concatenate([edge, above]) + jnp.concatenate([below, edge])
        if j == 0:
            part = jnp.where(column == 0, 0.0, pltpu.roll(part, 1, 0))
        if j == 2:
            part = jnp.where(column == cols - 1, 0.0, pltpu.roll(part, count - 1, 0))
        total = part if total is None else total + part
    activated = (total / (1.0 + jnp.exp(-total))).astype(BF16)
    out_ref[...] = dot(order_ref[...], activated).astype(BF16)


def temporal_kernel(plan, got_ref, own_ref, other_ref, out_ref):
    core = lax.rem(lax.axis_index("space"), CORES)
    half, depth = plan.send_rows // 2, plan.slice_chans
    row = lax.broadcasted_iota(jnp.int32, (plan.down_rows, 1), 0)
    first = (row & (plan.back - 1)) < plan.ncol
    total = None
    for index, weight_ref in ((core, own_ref), (1 - core, other_ref)):
        block = got_ref[:, index].astype(F32)
        even = block[:, :half].reshape(plan.down_rows, depth)
        odd = block[:, half:].reshape(plan.down_rows, depth)
        before = jnp.where(first, pltpu.roll(odd, half - plan.back + plan.ncol, 0), pltpu.roll(odd, plan.ncol, 0))
        for k, rows in enumerate((before, even, odd)):
            part = dot(rows.astype(BF16), weight_ref[k])
            total = part if total is None else total + part
    out_ref[...] = total.astype(BF16)


def turn_kernel(own_ref, other_ref, out_ref):
    kinds, depth, chans = own_ref.shape
    for k, ref in enumerate((own_ref, other_ref)):
        out_ref[k] = ref[...].reshape(kinds * depth, chans).T


def attend_kernel(plan, gain_ref, qkv_ref, own_out, other_out, *refs):
    down_refs, out_ref = refs[:-1], refs[-1]
    rows, depth = plan.down_rows, plan.slice_chans
    heads = depth // HD
    down = down_refs[0][...].astype(F32)
    for ref in down_refs[1:]:
        down = down + ref[...].astype(F32)
    down = down.astype(BF16).astype(F32)
    normed = rms_scale(down, gain_ref[...]).astype(BF16)
    channel_head = lax.broadcasted_iota(jnp.int32, (1, depth), 1) >> (HD.bit_length() - 1)
    key_head = lax.broadcasted_iota(jnp.int32, (1, heads * rows), 1) >> (rows.bit_length() - 1)
    key_row_head = lax.broadcasted_iota(jnp.int32, (heads * rows, 1), 0) >> (rows.bit_length() - 1)
    spread = jnp.where(key_row_head == channel_head, 1.0, 0.0).astype(BF16)

    def by_head(block):
        wide = block.astype(F32)
        return jnp.concatenate([jnp.where(channel_head == h, wide, 0.0) for h in range(heads)]).astype(BF16)

    def pixel(number):
        return (number & (plan.ncol - 1)) + ((number >> (plan.back.bit_length() - 1)) & (plan.x - 1)) * plan.ncol

    query_pixel = pixel(lax.broadcasted_iota(jnp.int32, (rows, 1), 0))
    key_pixel = pixel(lax.broadcasted_iota(jnp.int32, (1, heads * rows), 1) & (rows - 1))
    same = query_pixel == key_pixel
    first = lax.axis_index("space") < CORES
    projected = jnp.where(first, 1.0, 0.0) * down
    both = range(CORES)
    qkv = [dot(normed, qkv_ref[k]).astype(BF16) for k in both]
    keys = [by_head(qkv[k][:, depth : 2 * depth]) for k in both]
    values = [by_head(qkv[k][:, 2 * depth :]) for k in both]
    scores = [dot_trans(qkv[k][:, :depth], keys[k]) * (HD**-0.5) for k in both]
    weights = []
    for score in scores:
        score = jnp.where(same, score, -jnp.inf)
        top = None
        for h in range(heads):
            peak = jnp.max(jnp.where(key_head == h, score, -jnp.inf), axis=-1, keepdims=True)
            top = peak if h == 0 else jnp.where(key_head >= h, peak, top)
        weights.append(jnp.exp(score - top).astype(BF16))
    mixed = [(dot(w, v) / dot(w, spread)).astype(BF16) for w, v in zip(weights, values)]
    projected = projected + dot(mixed[0], own_out[...]) + dot(mixed[1], other_out[...])
    width = plan.back_width
    parts = [projected[:, k * width : (k + 1) * width] for k in range(plan.lanes)]
    parts = [part.reshape(plan.peers, plan.back, width) for part in parts]
    out_ref[...] = jnp.concatenate(parts, axis=1).reshape(plan.peers * plan.back_rows, width).astype(BF16)


def end_kernel(plan, got_ref, order_ref, latents_ref, out_ref):
    got = got_ref[...]
    bottom = [dot(order_ref[k], got) for k in range(plan.lanes)]
    bottom = jnp.concatenate(bottom, axis=1).astype(BF16).astype(F32)
    for f in range(plan.views):
        block = bottom[(f // 2) * plan.cols : (f // 2 + 1) * plan.cols]
        out_ref[f] = (latents_ref[f].astype(F32) + block).astype(BF16)


def call(kernel, name, shapes, args, scratch=(), flops=0, space=pltpu.VMEM):
    outs = [s if isinstance(s, jax.ShapeDtypeStruct) else jax.ShapeDtypeStruct(s, BF16) for s in shapes]
    moved = sum(a.size * a.dtype.itemsize for a in (*args, *outs))
    return pl.pallas_call(
        kernel,
        out_shape=outs,
        in_specs=[pl.BlockSpec(memory_space=space)] * len(args),
        out_specs=[pl.BlockSpec(memory_space=pltpu.VMEM)] * len(outs),
        scratch_shapes=list(scratch),
        compiler_params=pltpu.CompilerParams(vmem_limit_bytes=16 * 2**20),
        cost_estimate=pl.CostEstimate(flops=flops, bytes_accessed=moved, transcendentals=0),
        name=name,
    )(*args)


def body(latents, conv_gain, spatial_weight, temporal_weight, attn_gain, qkv_weight, out_weight):
    views, _, cols, chans = latents.shape
    orbit, space = lax.axis_size("orbit"), lax.axis_size("space")
    plan = Plan(orbit, space, views, cols, chans, spatial_weight.shape[2])
    conv_gain, attn_gain = conv_gain.reshape(1, chans), attn_gain.reshape(1, chans)

    def swap(block, distance):
        return lax.ppermute(block, "space", [(s, s ^ distance) for s in range(space)])

    def exchange(blocks, groups):
        return lax.all_to_all(blocks, ("orbit", "space"), 0, 0, tiled=True, axis_index_groups=groups)

    by_core = [[o * space + x * CORES + c for o in range(orbit) for c in range(CORES)] for x in range(plan.x)]
    by_x = [[o * space + x * CORES + c for o in range(orbit) for x in range(plan.x)] for c in range(CORES)]

    own = latents.reshape(views * cols, chans)
    far = [swap(own, x * CORES) for x in range(1, plan.x)]
    near = swap(own, 1)
    (normed,) = call(norm_kernel, "norm_own", [own.shape], (conv_gain, own), flops=60 * 10**9)
    far, near, normed = lax.optimization_barrier((far, near, normed))
    other_temporal, other_qkv, other_out = [swap(w, 1) for w in (temporal_weight, qkv_weight, out_weight)]
    across = [swap(block, 1) for block in far]
    ready = call(norm_kernel, "norm", [own.shape] * plan.x, (conv_gain, near, *far), flops=6 * 10**9)

    count = space * views * cols
    (activated,) = call(
        functools.partial(conv_kernel, plan),
        "conv",
        [(count, plan.slice_chans)],
        (conv_gain, spatial_weight, plan.send_order(), normed, *ready, *across),
        [pltpu.VMEM((space, views * cols, chans), BF16)],
        flops=2 * 9 * count * chans * plan.slice_chans,
    )
    swapped = (other_temporal, other_qkv, other_out)
    activated, (other_temporal, other_qkv, other_out) = lax.optimization_barrier((activated, swapped))
    got = exchange(activated.reshape(orbit * CORES, plan.send_rows, plan.slice_chans), by_core)
    (down,) = call(
        functools.partial(temporal_kernel, plan),
        "temporal",
        [(plan.down_rows, chans)],
        (got.reshape(orbit, CORES, plan.send_rows, plan.slice_chans), temporal_weight, other_temporal),
        flops=2 * 6 * plan.down_rows * chans * plan.slice_chans,
    )
    down, own_qkv, other_qkv = lax.optimization_barrier((down, qkv_weight, other_qkv))
    downs = [down] + [swap(down, x * CORES) for x in range(1, plan.x)]
    (qkv,) = call(
        turn_kernel,
        "turn",
        [(2, chans, 3 * plan.slice_chans)],
        (own_qkv, other_qkv),
        flops=6 * 10**9,
    )
    peers = plan.peers
    (back,) = call(
        functools.partial(attend_kernel, plan),
        "attend",
        [(peers * plan.back_rows, plan.back_width)],
        (attn_gain, qkv, out_weight, other_out, *downs),
        flops=2 * 8 * plan.down_rows * chans * plan.slice_chans,
    )
    got = exchange(back.reshape(peers, plan.back_rows, plan.back_width), by_x)
    (restored,) = call(
        functools.partial(end_kernel, plan),
        "restore",
        [(views, cols, chans)],
        (got.reshape(peers * plan.back_rows, plan.back_width), plan.end_order(), latents.reshape(views, cols, chans)),
    )
    return restored.reshape(latents.shape)


def solution(mesh):
    return jax.shard_map(
        body,
        mesh=mesh,
        in_specs=(
            P("orbit", "space", None, None),
            P(),
            P(None, None, "space", None),
            P(None, "space", None),
            P(),
            P(None, "space", None),
            P("space", None),
        ),
        out_specs=P("orbit", "space", None, None),
        check_vma=False,
    )
```

```python
import functools

import jax
import jax.numpy as jnp
import numpy as np
from jax import lax
from jax.experimental import pallas as pl
from jax.experimental.pallas import tpu as pltpu
from jax.sharding import PartitionSpec as P

HD = 64
CORES = 2
F32 = jnp.float32
BF16 = jnp.bfloat16


def dot(left, right):
    return jnp.dot(left, right, preferred_element_type=F32)


def dot_trans(left, right):
    return lax.dot_general(left, right, (((1,), (1,)), ((), ())), preferred_element_type=F32)


def rms_scale(wide, gain):
    return wide * lax.rsqrt(jnp.mean(wide * wide, axis=-1, keepdims=True) + 1e-06) * gain


def picks(source, width):
    return jnp.asarray(np.asarray(source).reshape(-1, 1) == np.arange(width), BF16)


class Plan:
    def __init__(self, orbit, space, views, cols, chans, slice_chans):
        self.orbit, self.space, self.views = orbit, space, views
        self.cols, self.chans, self.slice_chans = cols, chans, slice_chans
        self.x = space // CORES
        share = cols // orbit
        self.by_column = share % CORES == 0
        self.ncol = share // CORES if self.by_column else share
        self.rows = space if self.by_column else self.x
        self.pixels = self.rows * self.ncol
        self.pairs = views // 2
        self.down_rows = self.pairs * orbit * self.pixels
        self.send_rows = views * self.pixels
        self.peers = orbit * self.rows
        self.back = self.pairs * self.ncol
        self.lanes = next(n for n in (1, 2, 4, 8) if self.back * n % 8 == 0)
        self.back_rows, self.back_width = self.back * self.lanes, chans // self.lanes

    def column(self, o, core, c):
        return (o * CORES + core) * self.ncol + c if self.by_column else o * self.ncol + c

    def send_order(self):
        o, core, odd, r, pair, c = np.indices((self.orbit, CORES, 2, self.rows, self.pairs, self.ncol))
        row = r if self.by_column else r * CORES + core
        source = (row * self.views + 2 * pair + odd) * self.cols + self.column(o, core, c)
        return picks(source, self.space * self.views * self.cols)

    def end_order(self):
        o, s, lane, view, c = np.indices((self.orbit, self.rows, self.lanes, self.pairs, self.ncol))
        target = (lane * self.pairs + view) * self.cols + self.column(o, s % CORES, c)
        count = self.lanes * self.pairs * self.cols
        return jnp.asarray(target.reshape(1, -1) == np.arange(count).reshape(-1, 1), BF16)


def norm_kernel(gain_ref, *refs):
    count = len(refs) // 2
    for x_ref, out_ref in zip(refs[:count], refs[count:]):
        out_ref[...] = rms_scale(x_ref[...].astype(F32), gain_ref[...]).astype(BF16)


def conv_kernel(plan, gain_ref, weight_ref, order_ref, *refs):
    x_refs, (out_ref, normed) = refs[:-2], refs[-2:]
    per_row, cols, depth = plan.views * plan.cols, plan.cols, plan.slice_chans
    gain = gain_ref[...]
    space = lax.axis_index("space")
    ready = plan.x + 1
    for k, x_ref in enumerate(x_refs):
        block = x_ref[...]
        if k >= ready:
            block = rms_scale(block.astype(F32), gain).astype(BF16)
        index = k if k < 2 else (k - 1) * CORES if k < ready else (k - ready + 1) * CORES + 1
        normed[space ^ index] = block
    count = plan.space * per_row
    rows = normed[...].reshape(count, plan.chans)
    column = lax.broadcasted_iota(jnp.int32, (count, 1), 0) & (cols - 1)
    total = None
    for j in (1, 0, 2):
        part = dot_trans(rows, weight_ref[1, j])
        above = dot_trans(rows[: count - per_row], weight_ref[0, j])
        below = dot_trans(rows[per_row:], weight_ref[2, j])
        edge = jnp.zeros((per_row, depth), F32)
        part = part + jnp.concatenate([edge, above]) + jnp.concatenate([below, edge])
        if j == 0:
            part = jnp.where(column == 0, 0.0, pltpu.roll(part, 1, 0))
        if j == 2:
            part = jnp.where(column == cols - 1, 0.0, pltpu.roll(part, count - 1, 0))
        total = part if total is None else total + part
    activated = (total / (1.0 + jnp.exp(-total))).astype(BF16)
    out_ref[...] = dot(order_ref[...], activated).astype(BF16)


def temporal_kernel(plan, got_ref, own_ref, other_ref, out_ref):
    core = lax.rem(lax.axis_index("space"), CORES)
    half, depth = plan.send_rows // 2, plan.slice_chans
    row = lax.broadcasted_iota(jnp.int32, (plan.down_rows, 1), 0)
    first = (row & (plan.back - 1)) < plan.ncol
    total = None
    for index, weight_ref in ((core, own_ref), (1 - core, other_ref)):
        block = got_ref[:, index].astype(F32)
        even = block[:, :half].reshape(plan.down_rows, depth)
        odd = block[:, half:].reshape(plan.down_rows, depth)
        before = jnp.where(first, pltpu.roll(odd, half - plan.back + plan.ncol, 0), pltpu.roll(odd, plan.ncol, 0))
        for k, rows in enumerate((before, even, odd)):
            part = dot(rows.astype(BF16), weight_ref[k])
            total = part if total is None else total + part
    out_ref[...] = total.astype(BF16)


def turn_kernel(own_ref, other_ref, out_ref):
    kinds, depth, chans = own_ref.shape
    for k, ref in enumerate((own_ref, other_ref)):
        out_ref[k] = ref[...].reshape(kinds * depth, chans).T


def attend_kernel(plan, gain_ref, qkv_ref, own_out, other_out, *refs):
    down_refs, out_ref = refs[:-1], refs[-1]
    rows, depth = plan.down_rows, plan.slice_chans
    heads = depth // HD
    down = down_refs[0][...].astype(F32)
    for ref in down_refs[1:]:
        down = down + ref[...].astype(F32)
    down = down.astype(BF16).astype(F32)
    normed = rms_scale(down, gain_ref[...]).astype(BF16)
    channel_head = lax.broadcasted_iota(jnp.int32, (1, depth), 1) >> (HD.bit_length() - 1)
    key_head = lax.broadcasted_iota(jnp.int32, (1, heads * rows), 1) >> (rows.bit_length() - 1)
    key_row_head = lax.broadcasted_iota(jnp.int32, (heads * rows, 1), 0) >> (rows.bit_length() - 1)
    spread = jnp.where(key_row_head == channel_head, 1.0, 0.0).astype(BF16)

    def by_head(block):
        wide = block.astype(F32)
        return jnp.concatenate([jnp.where(channel_head == h, wide, 0.0) for h in range(heads)]).astype(BF16)

    def pixel(number):
        return (number & (plan.ncol - 1)) + ((number >> (plan.back.bit_length() - 1)) & (plan.rows - 1)) * plan.ncol

    query_pixel = pixel(lax.broadcasted_iota(jnp.int32, (rows, 1), 0))
    key_pixel = pixel(lax.broadcasted_iota(jnp.int32, (1, heads * rows), 1) & (rows - 1))
    same = query_pixel == key_pixel
    first = lax.axis_index("space") < CORES
    projected = jnp.where(first, 1.0, 0.0) * down
    both = range(CORES)
    qkv = [dot(normed, qkv_ref[k]).astype(BF16) for k in both]
    keys = [by_head(qkv[k][:, depth : 2 * depth]) for k in both]
    values = [by_head(qkv[k][:, 2 * depth :]) for k in both]
    scores = [dot_trans(qkv[k][:, :depth], keys[k]) * (HD**-0.5) for k in both]
    weights = []
    for score in scores:
        score = jnp.where(same, score, -jnp.inf)
        top = None
        for h in range(heads):
            peak = jnp.max(jnp.where(key_head == h, score, -jnp.inf), axis=-1, keepdims=True)
            top = peak if h == 0 else jnp.where(key_head >= h, peak, top)
        weights.append(jnp.exp(score - top).astype(BF16))
    mixed = [(dot(w, v) / dot(w, spread)).astype(BF16) for w, v in zip(weights, values)]
    projected = projected + dot(mixed[0], own_out[...]) + dot(mixed[1], other_out[...])
    width = plan.back_width
    parts = [projected[:, k * width : (k + 1) * width] for k in range(plan.lanes)]
    parts = [part.reshape(plan.peers, plan.back, width) for part in parts]
    out_ref[...] = jnp.concatenate(parts, axis=1).reshape(plan.peers * plan.back_rows, width).astype(BF16)


def end_kernel(plan, got_ref, order_ref, latents_ref, out_ref):
    rows = plan.pairs * plan.cols
    bottom = dot(order_ref[...], got_ref[...])
    bottom = jnp.concatenate([bottom[k * rows : (k + 1) * rows] for k in range(plan.lanes)], axis=1)
    bottom = bottom.astype(BF16).astype(F32)
    for f in range(plan.views):
        block = bottom[(f // 2) * plan.cols : (f // 2 + 1) * plan.cols]
        out_ref[f] = (latents_ref[f].astype(F32) + block).astype(BF16)


def call(kernel, name, shapes, args, scratch=(), flops=0, space=pltpu.VMEM):
    outs = [s if isinstance(s, jax.ShapeDtypeStruct) else jax.ShapeDtypeStruct(s, BF16) for s in shapes]
    moved = sum(a.size * a.dtype.itemsize for a in (*args, *outs))
    return pl.pallas_call(
        kernel,
        out_shape=outs,
        in_specs=[pl.BlockSpec(memory_space=space)] * len(args),
        out_specs=[pl.BlockSpec(memory_space=pltpu.VMEM)] * len(outs),
        scratch_shapes=list(scratch),
        compiler_params=pltpu.CompilerParams(vmem_limit_bytes=16 * 2**20),
        cost_estimate=pl.CostEstimate(flops=flops, bytes_accessed=moved, transcendentals=0),
        name=name,
    )(*args)


def body(latents, conv_gain, spatial_weight, temporal_weight, attn_gain, qkv_weight, out_weight):
    views, _, cols, chans = latents.shape
    orbit, space = lax.axis_size("orbit"), lax.axis_size("space")
    plan = Plan(orbit, space, views, cols, chans, spatial_weight.shape[2])
    conv_gain, attn_gain = conv_gain.reshape(1, chans), attn_gain.reshape(1, chans)

    def swap(block, distance):
        return lax.ppermute(block, "space", [(s, s ^ distance) for s in range(space)])

    def exchange(blocks, groups):
        return lax.all_to_all(blocks, ("orbit", "space"), 0, 0, tiled=True, axis_index_groups=groups)

    by_core = [[o * space + x * CORES + c for o in range(orbit) for c in range(CORES)] for x in range(plan.x)]
    by_x = [[o * space + x * CORES + c for o in range(orbit) for x in range(plan.x)] for c in range(CORES)]

    own = latents.reshape(views * cols, chans)
    far = [swap(own, x * CORES) for x in range(1, plan.x)]
    near = swap(own, 1)
    (normed,) = call(norm_kernel, "norm_own", [own.shape], (conv_gain, own), flops=60 * 10**9)
    far, near, normed = lax.optimization_barrier((far, near, normed))
    other_temporal, other_qkv, other_out = [swap(w, 1) for w in (temporal_weight, qkv_weight, out_weight)]
    across = [swap(block, 1) for block in far]
    ready = call(norm_kernel, "norm", [own.shape] * plan.x, (conv_gain, near, *far), flops=6 * 10**9)

    count = space * views * cols
    (activated,) = call(
        functools.partial(conv_kernel, plan),
        "conv",
        [(count, plan.slice_chans)],
        (conv_gain, spatial_weight, plan.send_order(), normed, *ready, *across),
        [pltpu.VMEM((space, views * cols, chans), BF16)],
        flops=2 * 9 * count * chans * plan.slice_chans,
    )
    swapped = (other_temporal, other_qkv, other_out)
    activated, (other_temporal, other_qkv, other_out) = lax.optimization_barrier((activated, swapped))
    got = exchange(activated.reshape(orbit * CORES, plan.send_rows, plan.slice_chans), by_core)
    (down,) = call(
        functools.partial(temporal_kernel, plan),
        "temporal",
        [(plan.down_rows, chans)],
        (got.reshape(orbit, CORES, plan.send_rows, plan.slice_chans), temporal_weight, other_temporal),
        flops=2 * 6 * plan.down_rows * chans * plan.slice_chans,
    )
    down, own_qkv, other_qkv = lax.optimization_barrier((down, qkv_weight, other_qkv))
    downs = [down] + [swap(down, x * CORES) for x in range(1, plan.x)]
    (qkv,) = call(
        turn_kernel,
        "turn",
        [(2, chans, 3 * plan.slice_chans)],
        (own_qkv, other_qkv),
        flops=6 * 10**9,
    )
    peers = plan.peers
    (back,) = call(
        functools.partial(attend_kernel, plan),
        "attend",
        [(peers * plan.back_rows, plan.back_width)],
        (attn_gain, qkv, out_weight, other_out, *downs),
        flops=2 * 8 * plan.down_rows * chans * plan.slice_chans,
    )
    got = exchange(back.reshape(peers, plan.back_rows, plan.back_width), None if plan.by_column else by_x)
    (restored,) = call(
        functools.partial(end_kernel, plan),
        "restore",
        [(views, cols, chans)],
        (got.reshape(peers * plan.back_rows, plan.back_width), plan.end_order(), latents.reshape(views, cols, chans)),
    )
    return restored.reshape(latents.shape)


def solution(mesh):
    return jax.shard_map(
        body,
        mesh=mesh,
        in_specs=(
            P("orbit", "space", None, None),
            P(),
            P(None, None, "space", None),
            P(None, "space", None),
            P(),
            P(None, "space", None),
            P("space", None),
        ),
        out_specs=P("orbit", "space", None, None),
        check_vma=False,
    )
```

```python
import functools

import jax
import jax.numpy as jnp
import numpy as np
from jax import lax
from jax.experimental import pallas as pl
from jax.experimental.pallas import tpu as pltpu
from jax.sharding import PartitionSpec as P

HD = 64
CORES = 2
F32 = jnp.float32
BF16 = jnp.bfloat16


def dot(left, right):
    return jnp.dot(left, right, preferred_element_type=F32)


def dot_trans(left, right):
    return lax.dot_general(left, right, (((1,), (1,)), ((), ())), preferred_element_type=F32)


def rms_scale(wide, gain):
    return wide * lax.rsqrt(jnp.mean(wide * wide, axis=-1, keepdims=True) + 1e-06) * gain


def picks(source, width):
    return jnp.asarray(np.asarray(source).reshape(-1, 1) == np.arange(width), BF16)


class Plan:
    def __init__(self, orbit, space, views, cols, chans, slice_chans):
        self.orbit, self.space, self.views = orbit, space, views
        self.cols, self.chans, self.slice_chans = cols, chans, slice_chans
        self.x = space // CORES
        share = cols // orbit
        self.by_column = share % CORES == 0
        self.ncol = share // CORES if self.by_column else share
        self.rows = space if self.by_column else self.x
        self.pixels = self.rows * self.ncol
        self.pairs = views // 2
        self.down_rows = self.pairs * orbit * self.pixels
        self.send_rows = views * self.pixels
        self.peers = orbit * self.rows
        self.back = self.pairs * self.ncol
        self.lanes = next(n for n in (1, 2, 4, 8) if self.back * n % 8 == 0)
        self.back_rows, self.back_width = self.back * self.lanes, chans // self.lanes

    def column(self, o, core, c):
        return (o * CORES + core) * self.ncol + c if self.by_column else o * self.ncol + c

    def send_order(self):
        o, core, odd, r, pair, c = np.indices((self.orbit, CORES, 2, self.rows, self.pairs, self.ncol))
        row = r if self.by_column else r * CORES + core
        source = (row * self.views + 2 * pair + odd) * self.cols + self.column(o, core, c)
        return picks(source, self.space * self.views * self.cols)

    def end_order(self):
        o, s, lane, view, c = np.indices((self.orbit, self.rows, self.lanes, self.pairs, self.ncol))
        target = (lane * self.pairs + view) * self.cols + self.column(o, s % CORES, c)
        count = self.lanes * self.pairs * self.cols
        return jnp.asarray(target.reshape(1, -1) == np.arange(count).reshape(-1, 1), BF16)


def norm_kernel(gain_ref, *refs):
    count = len(refs) // 2
    for x_ref, out_ref in zip(refs[:count], refs[count:]):
        out_ref[...] = rms_scale(x_ref[...].astype(F32), gain_ref[...]).astype(BF16)


def conv_kernel(plan, gain_ref, weight_ref, order_ref, *refs):
    x_refs, (out_ref, normed) = refs[:-2], refs[-2:]
    per_row, cols, depth = plan.views * plan.cols, plan.cols, plan.slice_chans
    gain = gain_ref[...]
    space = lax.axis_index("space")
    ready = plan.x + 1
    for k, x_ref in enumerate(x_refs):
        block = x_ref[...]
        if k >= ready:
            block = rms_scale(block.astype(F32), gain).astype(BF16)
        index = k if k < 2 else (k - 1) * CORES if k < ready else (k - ready + 1) * CORES + 1
        normed[space ^ index] = block
    count = plan.space * per_row
    rows = normed[...].reshape(count, plan.chans)
    column = lax.broadcasted_iota(jnp.int32, (count, 1), 0) & (cols - 1)
    total = None
    for j in (1, 0, 2):
        part = dot_trans(rows, weight_ref[1, j])
        above = dot_trans(rows[: count - per_row], weight_ref[0, j])
        below = dot_trans(rows[per_row:], weight_ref[2, j])
        edge = jnp.zeros((per_row, depth), F32)
        part = part + jnp.concatenate([edge, above]) + jnp.concatenate([below, edge])
        if j == 0:
            part = jnp.where(column == 0, 0.0, pltpu.roll(part, 1, 0))
        if j == 2:
            part = jnp.where(column == cols - 1, 0.0, pltpu.roll(part, count - 1, 0))
        total = part if total is None else total + part
    activated = (total / (1.0 + jnp.exp(-total))).astype(BF16)
    out_ref[...] = dot(order_ref[...], activated).astype(BF16)


def temporal_kernel(plan, got_ref, own_ref, other_ref, out_ref):
    core = lax.rem(lax.axis_index("space"), CORES)
    half, depth = plan.send_rows // 2, plan.slice_chans
    row = lax.broadcasted_iota(jnp.int32, (plan.down_rows, 1), 0)
    first = (row & (plan.back - 1)) < plan.ncol
    total = None
    for index, weight_ref in ((core, own_ref), (1 - core, other_ref)):
        block = got_ref[:, index].astype(F32)
        even = block[:, :half].reshape(plan.down_rows, depth)
        odd = block[:, half:].reshape(plan.down_rows, depth)
        before = jnp.where(first, pltpu.roll(odd, half - plan.back + plan.ncol, 0), pltpu.roll(odd, plan.ncol, 0))
        for k, rows in enumerate((before, even, odd)):
            part = dot(rows.astype(BF16), weight_ref[k])
            total = part if total is None else total + part
    out_ref[...] = total.astype(BF16)


def turn_kernel(own_ref, other_ref, out_ref):
    kinds, depth, chans = own_ref.shape
    for k, ref in enumerate((own_ref, other_ref)):
        out_ref[k] = ref[...].reshape(kinds * depth, chans).T


def attend_kernel(plan, gain_ref, qkv_ref, own_out, other_out, *refs):
    down_refs, out_ref = refs[:-1], refs[-1]
    rows, depth = plan.down_rows, plan.slice_chans
    heads = depth // HD
    down = down_refs[0][...].astype(F32)
    for ref in down_refs[1:]:
        down = down + ref[...].astype(F32)
    down = down.astype(BF16).astype(F32)
    normed = rms_scale(down, gain_ref[...]).astype(BF16)
    channel_head = lax.broadcasted_iota(jnp.int32, (1, depth), 1) >> (HD.bit_length() - 1)
    key_head = lax.broadcasted_iota(jnp.int32, (1, heads * rows), 1) >> (rows.bit_length() - 1)
    key_row_head = lax.broadcasted_iota(jnp.int32, (heads * rows, 1), 0) >> (rows.bit_length() - 1)
    spread = jnp.where(key_row_head == channel_head, 1.0, 0.0).astype(BF16)

    def by_head(block):
        wide = block.astype(F32)
        return jnp.concatenate([jnp.where(channel_head == h, wide, 0.0) for h in range(heads)]).astype(BF16)

    def pixel(number):
        return (number & (plan.ncol - 1)) + ((number >> (plan.back.bit_length() - 1)) & (plan.rows - 1)) * plan.ncol

    query_pixel = pixel(lax.broadcasted_iota(jnp.int32, (rows, 1), 0))
    key_pixel = pixel(lax.broadcasted_iota(jnp.int32, (1, heads * rows), 1) & (rows - 1))
    same = query_pixel == key_pixel
    first = lax.axis_index("space") < CORES
    projected = jnp.where(first, 1.0, 0.0) * down
    both = range(CORES)
    qkv = [dot(normed, qkv_ref[k]).astype(BF16) for k in both]
    keys = [by_head(qkv[k][:, depth : 2 * depth]) for k in both]
    values = [by_head(qkv[k][:, 2 * depth :]) for k in both]
    scores = [dot_trans(qkv[k][:, :depth], keys[k]) * (HD**-0.5) for k in both]
    weights = []
    for score in scores:
        score = jnp.where(same, score, -jnp.inf)
        top = None
        for h in range(heads):
            peak = jnp.max(jnp.where(key_head == h, score, -jnp.inf), axis=-1, keepdims=True)
            top = peak if h == 0 else jnp.where(key_head >= h, peak, top)
        weights.append(jnp.exp(score - top).astype(BF16))
    mixed = [(dot(w, v) / dot(w, spread)).astype(BF16) for w, v in zip(weights, values)]
    projected = projected + dot(mixed[0], own_out[...]) + dot(mixed[1], other_out[...])
    width = plan.back_width
    parts = [projected[:, k * width : (k + 1) * width] for k in range(plan.lanes)]
    parts = [part.reshape(plan.peers, plan.back, width) for part in parts]
    out_ref[...] = jnp.concatenate(parts, axis=1).reshape(plan.peers * plan.back_rows, width).astype(BF16)


def end_kernel(plan, got_ref, order_ref, latents_ref, out_ref):
    rows = plan.pairs * plan.cols
    bottom = dot(order_ref[...], got_ref[...])
    bottom = jnp.concatenate([bottom[k * rows : (k + 1) * rows] for k in range(plan.lanes)], axis=1)
    bottom = bottom.astype(BF16).astype(F32)
    for f in range(plan.views):
        block = bottom[(f // 2) * plan.cols : (f // 2 + 1) * plan.cols]
        out_ref[f] = (latents_ref[f].astype(F32) + block).astype(BF16)


def call(kernel, name, shapes, args, scratch=(), flops=0, space=pltpu.VMEM):
    outs = [s if isinstance(s, jax.ShapeDtypeStruct) else jax.ShapeDtypeStruct(s, BF16) for s in shapes]
    moved = sum(a.size * a.dtype.itemsize for a in (*args, *outs))
    return pl.pallas_call(
        kernel,
        out_shape=outs,
        in_specs=[pl.BlockSpec(memory_space=space)] * len(args),
        out_specs=[pl.BlockSpec(memory_space=pltpu.VMEM)] * len(outs),
        scratch_shapes=list(scratch),
        compiler_params=pltpu.CompilerParams(vmem_limit_bytes=16 * 2**20),
        cost_estimate=pl.CostEstimate(flops=flops, bytes_accessed=moved, transcendentals=0),
        name=name,
    )(*args)


def body(latents, conv_gain, spatial_weight, temporal_weight, attn_gain, qkv_weight, out_weight):
    views, _, cols, chans = latents.shape
    orbit, space = lax.axis_size("orbit"), lax.axis_size("space")
    plan = Plan(orbit, space, views, cols, chans, spatial_weight.shape[2])
    conv_gain, attn_gain = conv_gain.reshape(1, chans), attn_gain.reshape(1, chans)

    def swap(block, distance):
        return lax.ppermute(block, "space", [(s, s ^ distance) for s in range(space)])

    def exchange(blocks, groups):
        return lax.all_to_all(blocks, ("orbit", "space"), 0, 0, tiled=True, axis_index_groups=groups)

    by_core = [[o * space + x * CORES + c for o in range(orbit) for c in range(CORES)] for x in range(plan.x)]
    by_x = [[o * space + x * CORES + c for o in range(orbit) for x in range(plan.x)] for c in range(CORES)]

    own = latents.reshape(views * cols, chans)
    far = [swap(own, x * CORES) for x in range(1, plan.x)]
    near = swap(own, 1)
    (normed,) = call(norm_kernel, "norm_own", [own.shape], (conv_gain, own), flops=60 * 10**9)
    far, near, normed = lax.optimization_barrier((far, near, normed))
    other_temporal, other_out = swap(temporal_weight, 1), swap(out_weight, 1)
    across = [swap(block, 1) for block in far]
    ready = call(norm_kernel, "norm", [own.shape] * plan.x, (conv_gain, near, *far), flops=6 * 10**9)

    count = space * views * cols
    (activated,) = call(
        functools.partial(conv_kernel, plan),
        "conv",
        [(count, plan.slice_chans)],
        (conv_gain, spatial_weight, plan.send_order(), normed, *ready, *across),
        [pltpu.VMEM((space, views * cols, chans), BF16)],
        flops=2 * 9 * count * chans * plan.slice_chans,
    )
    swapped = (other_temporal, other_out)
    activated, swapped, qkv = lax.optimization_barrier((activated, swapped, qkv_weight))
    (other_temporal, other_out), other_qkv = swapped, swap(qkv, 1)
    got = exchange(activated.reshape(orbit * CORES, plan.send_rows, plan.slice_chans), by_core)
    (down,) = call(
        functools.partial(temporal_kernel, plan),
        "temporal",
        [(plan.down_rows, chans)],
        (got.reshape(orbit, CORES, plan.send_rows, plan.slice_chans), temporal_weight, other_temporal),
        flops=2 * 6 * plan.down_rows * chans * plan.slice_chans,
    )
    down, own_qkv, other_qkv = lax.optimization_barrier((down, qkv_weight, other_qkv))
    downs = [down] + [swap(down, x * CORES) for x in range(1, plan.x)]
    (qkv,) = call(
        turn_kernel,
        "turn",
        [(2, chans, 3 * plan.slice_chans)],
        (own_qkv, other_qkv),
        flops=6 * 10**9,
    )
    peers = plan.peers
    (back,) = call(
        functools.partial(attend_kernel, plan),
        "attend",
        [(peers * plan.back_rows, plan.back_width)],
        (attn_gain, qkv, out_weight, other_out, *downs),
        flops=2 * 8 * plan.down_rows * chans * plan.slice_chans,
    )
    got = exchange(back.reshape(peers, plan.back_rows, plan.back_width), None if plan.by_column else by_x)
    (restored,) = call(
        functools.partial(end_kernel, plan),
        "restore",
        [(views, cols, chans)],
        (got.reshape(peers * plan.back_rows, plan.back_width), plan.end_order(), latents.reshape(views, cols, chans)),
    )
    return restored.reshape(latents.shape)


def solution(mesh):
    return jax.shard_map(
        body,
        mesh=mesh,
        in_specs=(
            P("orbit", "space", None, None),
            P(),
            P(None, None, "space", None),
            P(None, "space", None),
            P(),
            P(None, "space", None),
            P("space", None),
        ),
        out_specs=P("orbit", "space", None, None),
        check_vma=False,
    )
```

```python
import functools

import jax
import jax.numpy as jnp
import numpy as np
from jax import lax
from jax.experimental import pallas as pl
from jax.experimental.pallas import tpu as pltpu
from jax.sharding import PartitionSpec as P

HD = 64
CORES = 2
F32 = jnp.float32
BF16 = jnp.bfloat16


def dot(left, right):
    return jnp.dot(left, right, preferred_element_type=F32)


def dot_trans(left, right):
    return lax.dot_general(left, right, (((1,), (1,)), ((), ())), preferred_element_type=F32)


def rms_scale(wide, gain):
    return wide * lax.rsqrt(jnp.mean(wide * wide, axis=-1, keepdims=True) + 1e-06) * gain


def picks(source, width):
    return jnp.asarray(np.asarray(source).reshape(-1, 1) == np.arange(width), BF16)


class Plan:
    def __init__(self, orbit, space, views, cols, chans, slice_chans):
        self.orbit, self.space, self.views = orbit, space, views
        self.cols, self.chans, self.slice_chans = cols, chans, slice_chans
        self.x = space // CORES
        share = cols // orbit
        self.by_column = share % CORES == 0
        self.ncol = share // CORES if self.by_column else share
        self.rows = space if self.by_column else self.x
        self.pixels = self.rows * self.ncol
        self.pairs = views // 2
        self.down_rows = self.pairs * orbit * self.pixels
        self.send_rows = views * self.pixels
        self.peers = orbit * self.rows
        self.back = self.pairs * self.ncol
        self.lanes = next(n for n in (1, 2, 4, 8) if self.back * n % 8 == 0)
        self.back_rows, self.back_width = self.back * self.lanes, chans // self.lanes

    def column(self, o, core, c):
        return (o * CORES + core) * self.ncol + c if self.by_column else o * self.ncol + c

    def send_order(self):
        o, core, odd, r, pair, c = np.indices((self.orbit, CORES, 2, self.rows, self.pairs, self.ncol))
        row = r if self.by_column else r * CORES + core
        source = (row * self.views + 2 * pair + odd) * self.cols + self.column(o, core, c)
        return picks(source, self.space * self.views * self.cols)

    def end_order(self):
        o, s, lane, view, c = np.indices((self.orbit, self.rows, self.lanes, self.pairs, self.ncol))
        target = (lane * self.pairs + view) * self.cols + self.column(o, s % CORES, c)
        count = self.lanes * self.pairs * self.cols
        return jnp.asarray(target.reshape(1, -1) == np.arange(count).reshape(-1, 1), BF16)


def turn_conv_kernel(weight_ref, out_ref):
    taps, _, depth, chans = weight_ref.shape
    for i in range(taps):
        out_ref[i] = weight_ref[i].reshape(taps * depth, chans).T


def add_rows(plan, blocks, places, weight_ref, total):
    per_row, cols, depth = plan.views * plan.cols, plan.cols, plan.slice_chans
    rows = jnp.concatenate(blocks)
    count = rows.shape[0]
    column = lax.broadcasted_iota(jnp.int32, (count, 1), 0) & (cols - 1)
    for i in range(3):
        part = dot(rows, weight_ref[i])
        left, middle, right = [part[:, j * depth : (j + 1) * depth] for j in range(3)]
        left = jnp.where(column == 0, 0.0, pltpu.roll(left, 1, 0))
        right = jnp.where(column == cols - 1, 0.0, pltpu.roll(right, count - 1, 0))
        part = left + middle + right
        for n, place in enumerate(places):
            total[place + 2 - i] += part[n * per_row : (n + 1) * per_row]


def early_kernel(plan, gain_ref, weight_ref, *refs):
    raw_refs, total_ref = refs[:-1], refs[-1]
    gain, space = gain_ref[...], lax.axis_index("space")
    blocks = [rms_scale(ref[...].astype(F32), gain).astype(BF16) for ref in raw_refs]
    places = [space, space ^ 1] + [space ^ (x * CORES) for x in range(1, plan.x)]
    total_ref[...] = jnp.zeros_like(total_ref)
    add_rows(plan, blocks, places, weight_ref, total_ref)


def late_kernel(plan, gain_ref, weight_ref, order_ref, early_ref, *refs):
    raw_refs, (out_ref, total) = refs[:-2], refs[-2:]
    gain, space = gain_ref[...], lax.axis_index("space")
    blocks = [rms_scale(ref[...].astype(F32), gain).astype(BF16) for ref in raw_refs]
    places = [space ^ (x * CORES + 1) for x in range(1, plan.x)]
    total[...] = early_ref[...]
    add_rows(plan, blocks, places, weight_ref, total)
    whole = total[1 : plan.space + 1].reshape(plan.space * plan.views * plan.cols, plan.slice_chans)
    activated = (whole / (1.0 + jnp.exp(-whole))).astype(BF16)
    out_ref[...] = dot(order_ref[...], activated).astype(BF16)


def temporal_kernel(plan, got_ref, own_ref, other_ref, out_ref):
    core = lax.rem(lax.axis_index("space"), CORES)
    half, depth = plan.send_rows // 2, plan.slice_chans
    row = lax.broadcasted_iota(jnp.int32, (plan.down_rows, 1), 0)
    first = (row & (plan.back - 1)) < plan.ncol
    total = None
    for index, weight_ref in ((core, own_ref), (1 - core, other_ref)):
        block = got_ref[:, index].astype(F32)
        even = block[:, :half].reshape(plan.down_rows, depth)
        odd = block[:, half:].reshape(plan.down_rows, depth)
        before = jnp.where(first, pltpu.roll(odd, half - plan.back + plan.ncol, 0), pltpu.roll(odd, plan.ncol, 0))
        for k, rows in enumerate((before, even, odd)):
            part = dot(rows.astype(BF16), weight_ref[k])
            total = part if total is None else total + part
    out_ref[...] = total.astype(BF16)


def turn_kernel(own_ref, other_ref, out_ref):
    kinds, depth, chans = own_ref.shape
    for k, ref in enumerate((own_ref, other_ref)):
        out_ref[k] = ref[...].reshape(kinds * depth, chans).T


def attend_kernel(plan, gain_ref, qkv_ref, own_out, other_out, *refs):
    down_refs, out_ref = refs[:-1], refs[-1]
    rows, depth = plan.down_rows, plan.slice_chans
    heads = depth // HD
    down = down_refs[0][...].astype(F32)
    for ref in down_refs[1:]:
        down = down + ref[...].astype(F32)
    down = down.astype(BF16).astype(F32)
    normed = rms_scale(down, gain_ref[...]).astype(BF16)
    channel_head = lax.broadcasted_iota(jnp.int32, (1, depth), 1) >> (HD.bit_length() - 1)
    key_head = lax.broadcasted_iota(jnp.int32, (1, heads * rows), 1) >> (rows.bit_length() - 1)
    key_row_head = lax.broadcasted_iota(jnp.int32, (heads * rows, 1), 0) >> (rows.bit_length() - 1)
    spread = jnp.where(key_row_head == channel_head, 1.0, 0.0).astype(BF16)

    def by_head(block):
        wide = block.astype(F32)
        return jnp.concatenate([jnp.where(channel_head == h, wide, 0.0) for h in range(heads)]).astype(BF16)

    def pixel(number):
        return (number & (plan.ncol - 1)) + ((number >> (plan.back.bit_length() - 1)) & (plan.rows - 1)) * plan.ncol

    query_pixel = pixel(lax.broadcasted_iota(jnp.int32, (rows, 1), 0))
    key_pixel = pixel(lax.broadcasted_iota(jnp.int32, (1, heads * rows), 1) & (rows - 1))
    same = query_pixel == key_pixel
    first = lax.axis_index("space") < CORES
    projected = jnp.where(first, 1.0, 0.0) * down
    both = range(CORES)
    qkv = [dot(normed, qkv_ref[k]).astype(BF16) for k in both]
    keys = [by_head(qkv[k][:, depth : 2 * depth]) for k in both]
    values = [by_head(qkv[k][:, 2 * depth :]) for k in both]
    scores = [dot_trans(qkv[k][:, :depth], keys[k]) * (HD**-0.5) for k in both]
    weights = []
    for score in scores:
        score = jnp.where(same, score, -jnp.inf)
        top = None
        for h in range(heads):
            peak = jnp.max(jnp.where(key_head == h, score, -jnp.inf), axis=-1, keepdims=True)
            top = peak if h == 0 else jnp.where(key_head >= h, peak, top)
        weights.append(jnp.exp(score - top).astype(BF16))
    mixed = [(dot(w, v) / dot(w, spread)).astype(BF16) for w, v in zip(weights, values)]
    projected = projected + dot(mixed[0], own_out[...]) + dot(mixed[1], other_out[...])
    width = plan.back_width
    parts = [projected[:, k * width : (k + 1) * width] for k in range(plan.lanes)]
    parts = [part.reshape(plan.peers, plan.back, width) for part in parts]
    out_ref[...] = jnp.concatenate(parts, axis=1).reshape(plan.peers * plan.back_rows, width).astype(BF16)


def end_kernel(plan, got_ref, order_ref, latents_ref, out_ref):
    rows = plan.pairs * plan.cols
    bottom = dot(order_ref[...], got_ref[...])
    bottom = jnp.concatenate([bottom[k * rows : (k + 1) * rows] for k in range(plan.lanes)], axis=1)
    bottom = bottom.astype(BF16).astype(F32)
    for f in range(plan.views):
        block = bottom[(f // 2) * plan.cols : (f // 2 + 1) * plan.cols]
        out_ref[f] = (latents_ref[f].astype(F32) + block).astype(BF16)


def call(kernel, name, shapes, args, scratch=(), flops=0, space=pltpu.VMEM):
    outs = [s if isinstance(s, jax.ShapeDtypeStruct) else jax.ShapeDtypeStruct(s, BF16) for s in shapes]
    moved = sum(a.size * a.dtype.itemsize for a in (*args, *outs))
    return pl.pallas_call(
        kernel,
        out_shape=outs,
        in_specs=[pl.BlockSpec(memory_space=space)] * len(args),
        out_specs=[pl.BlockSpec(memory_space=pltpu.VMEM)] * len(outs),
        scratch_shapes=list(scratch),
        compiler_params=pltpu.CompilerParams(vmem_limit_bytes=16 * 2**20),
        cost_estimate=pl.CostEstimate(flops=flops, bytes_accessed=moved, transcendentals=0),
        name=name,
    )(*args)


def body(latents, conv_gain, spatial_weight, temporal_weight, attn_gain, qkv_weight, out_weight):
    views, _, cols, chans = latents.shape
    orbit, space = lax.axis_size("orbit"), lax.axis_size("space")
    plan = Plan(orbit, space, views, cols, chans, spatial_weight.shape[2])
    conv_gain, attn_gain = conv_gain.reshape(1, chans), attn_gain.reshape(1, chans)

    def swap(block, distance):
        return lax.ppermute(block, "space", [(s, s ^ distance) for s in range(space)])

    def exchange(blocks, groups):
        return lax.all_to_all(blocks, ("orbit", "space"), 0, 0, tiled=True, axis_index_groups=groups)

    by_core = [[o * space + x * CORES + c for o in range(orbit) for c in range(CORES)] for x in range(plan.x)]
    by_x = [[o * space + x * CORES + c for o in range(orbit) for x in range(plan.x)] for c in range(CORES)]

    own = latents.reshape(views * cols, chans)
    far = [swap(own, x * CORES) for x in range(1, plan.x)]
    near = swap(own, 1)
    depth, per_row = plan.slice_chans, views * cols
    (taps,) = call(turn_conv_kernel, "turn_conv", [(3, chans, 3 * depth)], (spatial_weight,), flops=60 * 10**9)
    other_temporal, other_out = swap(temporal_weight, 1), swap(out_weight, 1)
    far, near, taps = lax.optimization_barrier((far, near, taps))
    across = [swap(block, 1) for block in far]
    total_shape = (space + 2, per_row, depth)
    (early,) = call(
        functools.partial(early_kernel, plan),
        "conv_early",
        [jax.ShapeDtypeStruct(total_shape, F32)],
        (conv_gain, taps, own, near, *far),
        flops=6 * 10**9,
    )
    count = space * per_row
    (activated,) = call(
        functools.partial(late_kernel, plan),
        "conv_late",
        [(count, depth)],
        (conv_gain, taps, plan.send_order(), early, *across),
        [pltpu.VMEM(total_shape, F32)],
        flops=2 * 9 * count * chans * depth,
    )
    swapped = (other_temporal, other_out)
    activated, swapped, qkv = lax.optimization_barrier((activated, swapped, qkv_weight))
    (other_temporal, other_out), other_qkv = swapped, swap(qkv, 1)
    got = exchange(activated.reshape(orbit * CORES, plan.send_rows, plan.slice_chans), by_core)
    (down,) = call(
        functools.partial(temporal_kernel, plan),
        "temporal",
        [(plan.down_rows, chans)],
        (got.reshape(orbit, CORES, plan.send_rows, plan.slice_chans), temporal_weight, other_temporal),
        flops=2 * 6 * plan.down_rows * chans * plan.slice_chans,
    )
    down, own_qkv, other_qkv = lax.optimization_barrier((down, qkv_weight, other_qkv))
    downs = [down] + [swap(down, x * CORES) for x in range(1, plan.x)]
    (qkv,) = call(
        turn_kernel,
        "turn",
        [(2, chans, 3 * plan.slice_chans)],
        (own_qkv, other_qkv),
        flops=6 * 10**9,
    )
    peers = plan.peers
    (back,) = call(
        functools.partial(attend_kernel, plan),
        "attend",
        [(peers * plan.back_rows, plan.back_width)],
        (attn_gain, qkv, out_weight, other_out, *downs),
        flops=2 * 8 * plan.down_rows * chans * plan.slice_chans,
    )
    got = exchange(back.reshape(peers, plan.back_rows, plan.back_width), None if plan.by_column else by_x)
    (restored,) = call(
        functools.partial(end_kernel, plan),
        "restore",
        [(views, cols, chans)],
        (got.reshape(peers * plan.back_rows, plan.back_width), plan.end_order(), latents.reshape(views, cols, chans)),
    )
    return restored.reshape(latents.shape)


def solution(mesh):
    return jax.shard_map(
        body,
        mesh=mesh,
        in_specs=(
            P("orbit", "space", None, None),
            P(),
            P(None, None, "space", None),
            P(None, "space", None),
            P(),
            P(None, "space", None),
            P("space", None),
        ),
        out_specs=P("orbit", "space", None, None),
        check_vma=False,
    )
```

```python
import functools

import jax
import jax.numpy as jnp
import numpy as np
from jax import lax
from jax.experimental import pallas as pl
from jax.experimental.pallas import tpu as pltpu
from jax.sharding import PartitionSpec as P

HD = 64
CORES = 2
F32 = jnp.float32
BF16 = jnp.bfloat16


def dot(left, right):
    return jnp.dot(left, right, preferred_element_type=F32)


def dot_trans(left, right):
    return lax.dot_general(left, right, (((1,), (1,)), ((), ())), preferred_element_type=F32)


def rms(wide):
    return lax.rsqrt(jnp.mean(wide * wide, axis=-1, keepdims=True) + 1e-06)


def picks(source, width):
    return jnp.asarray(np.asarray(source).reshape(-1, 1) == np.arange(width), BF16)


class Plan:
    def __init__(self, orbit, space, views, cols, chans, slice_chans):
        self.orbit, self.space, self.views = orbit, space, views
        self.cols, self.chans, self.slice_chans = cols, chans, slice_chans
        self.x = space // CORES
        share = cols // orbit
        self.by_column = share % CORES == 0
        self.ncol = share // CORES if self.by_column else share
        self.rows = space if self.by_column else self.x
        self.pixels = self.rows * self.ncol
        self.pairs = views // 2
        self.down_rows = self.pairs * orbit * self.pixels
        self.send_rows = views * self.pixels
        self.peers = orbit * self.rows
        self.back = self.pairs * self.ncol
        self.lanes = next(n for n in (1, 2, 4, 8) if self.back * n % 8 == 0)
        self.back_rows, self.back_width = self.back * self.lanes, chans // self.lanes

    def column(self, o, core, c):
        return (o * CORES + core) * self.ncol + c if self.by_column else o * self.ncol + c

    def send_order(self):
        o, core, odd, r, pair, c = np.indices((self.orbit, CORES, 2, self.rows, self.pairs, self.ncol))
        row = r if self.by_column else r * CORES + core
        source = (row * self.views + 2 * pair + odd) * self.cols + self.column(o, core, c)
        return picks(source, self.space * self.views * self.cols)

    def end_order(self):
        o, s, lane, view, c = np.indices((self.orbit, self.rows, self.lanes, self.pairs, self.ncol))
        target = (lane * self.pairs + view) * self.cols + self.column(o, s % CORES, c)
        count = self.lanes * self.pairs * self.cols
        return jnp.asarray(target.reshape(1, -1) == np.arange(count).reshape(-1, 1), BF16)


def turn_conv_kernel(weight_ref, out_ref):
    taps, _, depth, chans = weight_ref.shape
    for i in range(taps):
        out_ref[i] = weight_ref[i].reshape(taps * depth, chans).T


def add_rows(plan, blocks, gain, places, weight_ref, total):
    per_row, cols, depth = plan.views * plan.cols, plan.cols, plan.slice_chans
    wide = jnp.concatenate([block.astype(F32) for block in blocks])
    count = wide.shape[0]
    rows, scale = (wide * gain).astype(BF16), rms(wide)
    column = lax.broadcasted_iota(jnp.int32, (count, 1), 0) & (cols - 1)
    for i in range(3):
        part = dot(rows, weight_ref[i])
        left, middle, right = [part[:, j * depth : (j + 1) * depth] for j in range(3)]
        left, right = left * scale, right * scale
        left = jnp.where(column == 0, 0.0, pltpu.roll(left, 1, 0))
        right = jnp.where(column == cols - 1, 0.0, pltpu.roll(right, count - 1, 0))
        part = left + middle * scale + right
        for n, place in enumerate(places):
            total[place + 2 - i] += part[n * per_row : (n + 1) * per_row]


def early_kernel(plan, gain_ref, weight_ref, *refs):
    raw_refs, total_ref = refs[:-1], refs[-1]
    space = lax.axis_index("space")
    blocks = [ref[...] for ref in raw_refs]
    places = [space, space ^ 1] + [space ^ (x * CORES) for x in range(1, plan.x)]
    total_ref[...] = jnp.zeros_like(total_ref)
    add_rows(plan, blocks, gain_ref[...], places, weight_ref, total_ref)


def late_kernel(plan, gain_ref, weight_ref, order_ref, early_ref, *refs):
    raw_refs, (out_ref, total) = refs[:-2], refs[-2:]
    space = lax.axis_index("space")
    blocks = [ref[...] for ref in raw_refs]
    places = [space ^ (x * CORES + 1) for x in range(1, plan.x)]
    total[...] = early_ref[...]
    add_rows(plan, blocks, gain_ref[...], places, weight_ref, total)
    whole = total[1 : plan.space + 1].reshape(plan.space * plan.views * plan.cols, plan.slice_chans)
    activated = (whole / (1.0 + jnp.exp(-whole))).astype(BF16)
    out_ref[...] = dot(order_ref[...], activated).astype(BF16)


def temporal_kernel(plan, got_ref, own_ref, other_ref, out_ref):
    core = lax.rem(lax.axis_index("space"), CORES)
    half, depth = plan.send_rows // 2, plan.slice_chans
    row = lax.broadcasted_iota(jnp.int32, (plan.down_rows, 1), 0)
    first = (row & (plan.back - 1)) < plan.ncol
    total = None
    for index, weight_ref in ((core, own_ref), (1 - core, other_ref)):
        block = got_ref[:, index].astype(F32)
        even = block[:, :half].reshape(plan.down_rows, depth)
        odd = block[:, half:].reshape(plan.down_rows, depth)
        before = jnp.where(first, pltpu.roll(odd, half - plan.back + plan.ncol, 0), pltpu.roll(odd, plan.ncol, 0))
        for k, rows in enumerate((before, even, odd)):
            part = dot(rows.astype(BF16), weight_ref[k])
            total = part if total is None else total + part
    out_ref[...] = total.astype(BF16)


def turn_kernel(own_ref, other_ref, out_ref):
    kinds, depth, chans = own_ref.shape
    for k, ref in enumerate((own_ref, other_ref)):
        out_ref[k] = ref[...].reshape(kinds * depth, chans).T


def attend_kernel(plan, gain_ref, qkv_ref, own_out, other_out, *refs):
    down_refs, out_ref = refs[:-1], refs[-1]
    rows, depth = plan.down_rows, plan.slice_chans
    heads = depth // HD
    down = down_refs[0][...].astype(F32)
    for ref in down_refs[1:]:
        down = down + ref[...].astype(F32)
    down = down.astype(BF16).astype(F32)
    gained, scale = (down * gain_ref[...]).astype(BF16), rms(down)
    channel_head = lax.broadcasted_iota(jnp.int32, (1, depth), 1) >> (HD.bit_length() - 1)
    key_head = lax.broadcasted_iota(jnp.int32, (1, heads * rows), 1) >> (rows.bit_length() - 1)
    key_row_head = lax.broadcasted_iota(jnp.int32, (heads * rows, 1), 0) >> (rows.bit_length() - 1)
    spread = jnp.where(key_row_head == channel_head, 1.0, 0.0).astype(BF16)

    def by_head(block):
        wide = block.astype(F32)
        return jnp.concatenate([jnp.where(channel_head == h, wide, 0.0) for h in range(heads)]).astype(BF16)

    def pixel(number):
        return (number & (plan.ncol - 1)) + ((number >> (plan.back.bit_length() - 1)) & (plan.rows - 1)) * plan.ncol

    query_pixel = pixel(lax.broadcasted_iota(jnp.int32, (rows, 1), 0))
    key_pixel = pixel(lax.broadcasted_iota(jnp.int32, (1, heads * rows), 1) & (rows - 1))
    same = query_pixel == key_pixel
    first = lax.axis_index("space") < CORES
    projected = jnp.where(first, 1.0, 0.0) * down
    both = range(CORES)
    qkv = [(dot(gained, qkv_ref[k]) * scale).astype(BF16) for k in both]
    keys = [by_head(qkv[k][:, depth : 2 * depth]) for k in both]
    values = [by_head(qkv[k][:, 2 * depth :]) for k in both]
    scores = [dot_trans(qkv[k][:, :depth], keys[k]) * (HD**-0.5) for k in both]
    weights = []
    for score in scores:
        score = jnp.where(same, score, -jnp.inf)
        top = None
        for h in range(heads):
            peak = jnp.max(jnp.where(key_head == h, score, -jnp.inf), axis=-1, keepdims=True)
            top = peak if h == 0 else jnp.where(key_head >= h, peak, top)
        weights.append(jnp.exp(score - top).astype(BF16))
    mixed = [(dot(w, v) / dot(w, spread)).astype(BF16) for w, v in zip(weights, values)]
    projected = projected + dot(mixed[0], own_out[...]) + dot(mixed[1], other_out[...])
    width = plan.back_width
    parts = [projected[:, k * width : (k + 1) * width] for k in range(plan.lanes)]
    parts = [part.reshape(plan.peers, plan.back, width) for part in parts]
    out_ref[...] = jnp.concatenate(parts, axis=1).reshape(plan.peers * plan.back_rows, width).astype(BF16)


def end_kernel(plan, got_ref, order_ref, latents_ref, out_ref):
    rows = plan.pairs * plan.cols
    bottom = dot(order_ref[...], got_ref[...])
    bottom = jnp.concatenate([bottom[k * rows : (k + 1) * rows] for k in range(plan.lanes)], axis=1)
    bottom = bottom.astype(BF16).astype(F32)
    for f in range(plan.views):
        block = bottom[(f // 2) * plan.cols : (f // 2 + 1) * plan.cols]
        out_ref[f] = (latents_ref[f].astype(F32) + block).astype(BF16)


def call(kernel, name, shapes, args, scratch=(), flops=0, space=pltpu.VMEM):
    outs = [s if isinstance(s, jax.ShapeDtypeStruct) else jax.ShapeDtypeStruct(s, BF16) for s in shapes]
    moved = sum(a.size * a.dtype.itemsize for a in (*args, *outs))
    return pl.pallas_call(
        kernel,
        out_shape=outs,
        in_specs=[pl.BlockSpec(memory_space=space)] * len(args),
        out_specs=[pl.BlockSpec(memory_space=pltpu.VMEM)] * len(outs),
        scratch_shapes=list(scratch),
        compiler_params=pltpu.CompilerParams(vmem_limit_bytes=16 * 2**20),
        cost_estimate=pl.CostEstimate(flops=flops, bytes_accessed=moved, transcendentals=0),
        name=name,
    )(*args)


def body(latents, conv_gain, spatial_weight, temporal_weight, attn_gain, qkv_weight, out_weight):
    views, _, cols, chans = latents.shape
    orbit, space = lax.axis_size("orbit"), lax.axis_size("space")
    plan = Plan(orbit, space, views, cols, chans, spatial_weight.shape[2])
    conv_gain, attn_gain = conv_gain.reshape(1, chans), attn_gain.reshape(1, chans)

    def swap(block, distance):
        return lax.ppermute(block, "space", [(s, s ^ distance) for s in range(space)])

    def exchange(blocks, groups):
        return lax.all_to_all(blocks, ("orbit", "space"), 0, 0, tiled=True, axis_index_groups=groups)

    by_core = [[o * space + x * CORES + c for o in range(orbit) for c in range(CORES)] for x in range(plan.x)]
    by_x = [[o * space + x * CORES + c for o in range(orbit) for x in range(plan.x)] for c in range(CORES)]

    own = latents.reshape(views * cols, chans)
    far = [swap(own, x * CORES) for x in range(1, plan.x)]
    near = swap(own, 1)
    depth, per_row = plan.slice_chans, views * cols
    (taps,) = call(turn_conv_kernel, "turn_conv", [(3, chans, 3 * depth)], (spatial_weight,), flops=60 * 10**9)
    other_temporal, other_out = swap(temporal_weight, 1), swap(out_weight, 1)
    far, near, taps = lax.optimization_barrier((far, near, taps))
    across = [swap(block, 1) for block in far]
    total_shape = (space + 2, per_row, depth)
    (early,) = call(
        functools.partial(early_kernel, plan),
        "conv_early",
        [jax.ShapeDtypeStruct(total_shape, F32)],
        (conv_gain, taps, own, near, *far),
        flops=6 * 10**9,
    )
    count = space * per_row
    (activated,) = call(
        functools.partial(late_kernel, plan),
        "conv_late",
        [(count, depth)],
        (conv_gain, taps, plan.send_order(), early, *across),
        [pltpu.VMEM(total_shape, F32)],
        flops=2 * 9 * count * chans * depth,
    )
    swapped = (other_temporal, other_out)
    activated, swapped, qkv = lax.optimization_barrier((activated, swapped, qkv_weight))
    (other_temporal, other_out), other_qkv = swapped, swap(qkv, 1)
    got = exchange(activated.reshape(orbit * CORES, plan.send_rows, plan.slice_chans), by_core)
    (down,) = call(
        functools.partial(temporal_kernel, plan),
        "temporal",
        [(plan.down_rows, chans)],
        (got.reshape(orbit, CORES, plan.send_rows, plan.slice_chans), temporal_weight, other_temporal),
        flops=2 * 6 * plan.down_rows * chans * plan.slice_chans,
    )
    down, own_qkv, other_qkv = lax.optimization_barrier((down, qkv_weight, other_qkv))
    downs = [down] + [swap(down, x * CORES) for x in range(1, plan.x)]
    (qkv,) = call(
        turn_kernel,
        "turn",
        [(2, chans, 3 * plan.slice_chans)],
        (own_qkv, other_qkv),
        flops=6 * 10**9,
    )
    peers = plan.peers
    (back,) = call(
        functools.partial(attend_kernel, plan),
        "attend",
        [(peers * plan.back_rows, plan.back_width)],
        (attn_gain, qkv, out_weight, other_out, *downs),
        flops=2 * 8 * plan.down_rows * chans * plan.slice_chans,
    )
    got = exchange(back.reshape(peers, plan.back_rows, plan.back_width), None if plan.by_column else by_x)
    (restored,) = call(
        functools.partial(end_kernel, plan),
        "restore",
        [(views, cols, chans)],
        (got.reshape(peers * plan.back_rows, plan.back_width), plan.end_order(), latents.reshape(views, cols, chans)),
    )
    return restored.reshape(latents.shape)


def solution(mesh):
    return jax.shard_map(
        body,
        mesh=mesh,
        in_specs=(
            P("orbit", "space", None, None),
            P(),
            P(None, None, "space", None),
            P(None, "space", None),
            P(),
            P(None, "space", None),
            P("space", None),
        ),
        out_specs=P("orbit", "space", None, None),
        check_vma=False,
    )
```

```python
import functools

import jax
import jax.numpy as jnp
import numpy as np
from jax import lax
from jax.experimental import pallas as pl
from jax.experimental.pallas import tpu as pltpu
from jax.sharding import PartitionSpec as P

HD = 64
CORES = 2
F32 = jnp.float32
BF16 = jnp.bfloat16


def dot(left, right):
    return jnp.dot(left, right, preferred_element_type=F32)


def dot_trans(left, right):
    return lax.dot_general(left, right, (((1,), (1,)), ((), ())), preferred_element_type=F32)


def rms(wide):
    return lax.rsqrt(jnp.mean(wide * wide, axis=-1, keepdims=True) + 1e-06)


def rms_scale(wide, gain):
    return wide * rms(wide) * gain


def picks(source, width):
    return jnp.asarray(np.asarray(source).reshape(-1, 1) == np.arange(width), BF16)


class Plan:
    def __init__(self, orbit, space, views, cols, chans, slice_chans):
        self.orbit, self.space, self.views = orbit, space, views
        self.cols, self.chans, self.slice_chans = cols, chans, slice_chans
        self.x = space // CORES
        share = cols // orbit
        self.by_column = share % CORES == 0
        self.ncol = share // CORES if self.by_column else share
        self.rows = space if self.by_column else self.x
        self.pixels = self.rows * self.ncol
        self.pairs = views // 2
        self.down_rows = self.pairs * orbit * self.pixels
        self.send_rows = views * self.pixels
        self.peers = orbit * self.rows
        self.back = self.pairs * self.ncol
        self.lanes = next(n for n in (1, 2, 4, 8) if self.back * n % 8 == 0)
        self.back_rows, self.back_width = self.back * self.lanes, chans // self.lanes

    def column(self, o, core, c):
        return (o * CORES + core) * self.ncol + c if self.by_column else o * self.ncol + c

    def send_order(self):
        o, core, odd, r, pair, c = np.indices((self.orbit, CORES, 2, self.rows, self.pairs, self.ncol))
        row = r if self.by_column else r * CORES + core
        source = (row * self.views + 2 * pair + odd) * self.cols + self.column(o, core, c)
        return picks(source, self.space * self.views * self.cols)

    def end_order(self):
        o, s, lane, view, c = np.indices((self.orbit, self.rows, self.lanes, self.pairs, self.ncol))
        target = (lane * self.pairs + view) * self.cols + self.column(o, s % CORES, c)
        count = self.lanes * self.pairs * self.cols
        return jnp.asarray(target.reshape(1, -1) == np.arange(count).reshape(-1, 1), BF16)


def turn_conv_kernel(weight_ref, out_ref):
    taps, _, depth, chans = weight_ref.shape
    for i in range(taps):
        out_ref[i] = weight_ref[i].reshape(taps * depth, chans).T


def add_rows(plan, blocks, places, weight_ref, total):
    per_row, cols, depth = plan.views * plan.cols, plan.cols, plan.slice_chans
    rows = jnp.concatenate(blocks)
    count = rows.shape[0]
    column = lax.broadcasted_iota(jnp.int32, (count, 1), 0) & (cols - 1)
    for i in range(3):
        part = dot(rows, weight_ref[i])
        left, middle, right = [part[:, j * depth : (j + 1) * depth] for j in range(3)]
        left = jnp.where(column == 0, 0.0, pltpu.roll(left, 1, 0))
        right = jnp.where(column == cols - 1, 0.0, pltpu.roll(right, count - 1, 0))
        part = left + middle + right
        for n, place in enumerate(places):
            total[place + 2 - i] += part[n * per_row : (n + 1) * per_row]


def early_kernel(plan, gain_ref, weight_ref, *refs):
    raw_refs, total_ref = refs[:-1], refs[-1]
    gain, space = gain_ref[...], lax.axis_index("space")
    blocks = [rms_scale(ref[...].astype(F32), gain).astype(BF16) for ref in raw_refs]
    places = [space, space ^ 1] + [space ^ (x * CORES) for x in range(1, plan.x)]
    total_ref[...] = jnp.zeros_like(total_ref)
    add_rows(plan, blocks, places, weight_ref, total_ref)


def late_kernel(plan, gain_ref, weight_ref, order_ref, early_ref, *refs):
    raw_refs, (out_ref, total) = refs[:-2], refs[-2:]
    gain, space = gain_ref[...], lax.axis_index("space")
    blocks = [rms_scale(ref[...].astype(F32), gain).astype(BF16) for ref in raw_refs]
    places = [space ^ (x * CORES + 1) for x in range(1, plan.x)]
    total[...] = early_ref[...]
    add_rows(plan, blocks, places, weight_ref, total)
    whole = total[1 : plan.space + 1].reshape(plan.space * plan.views * plan.cols, plan.slice_chans)
    activated = (whole / (1.0 + jnp.exp(-whole))).astype(BF16)
    out_ref[...] = dot(order_ref[...], activated).astype(BF16)


def temporal_kernel(plan, got_ref, own_ref, other_ref, out_ref):
    core = lax.rem(lax.axis_index("space"), CORES)
    half, depth = plan.send_rows // 2, plan.slice_chans
    row = lax.broadcasted_iota(jnp.int32, (plan.down_rows, 1), 0)
    first = (row & (plan.back - 1)) < plan.ncol
    total = None
    for index, weight_ref in ((core, own_ref), (1 - core, other_ref)):
        block = got_ref[:, index].astype(F32)
        even = block[:, :half].reshape(plan.down_rows, depth)
        odd = block[:, half:].reshape(plan.down_rows, depth)
        before = jnp.where(first, pltpu.roll(odd, half - plan.back + plan.ncol, 0), pltpu.roll(odd, plan.ncol, 0))
        for k, rows in enumerate((before, even, odd)):
            part = dot(rows.astype(BF16), weight_ref[k])
            total = part if total is None else total + part
    out_ref[...] = total.astype(BF16)


def turn_kernel(own_ref, other_ref, out_ref):
    kinds, depth, chans = own_ref.shape
    for k, ref in enumerate((own_ref, other_ref)):
        out_ref[k] = ref[...].reshape(kinds * depth, chans).T


def attend_kernel(plan, gain_ref, qkv_ref, own_out, other_out, *refs):
    down_refs, out_ref = refs[:-1], refs[-1]
    rows, depth = plan.down_rows, plan.slice_chans
    heads = depth // HD
    down = down_refs[0][...].astype(F32)
    for ref in down_refs[1:]:
        down = down + ref[...].astype(F32)
    down = down.astype(BF16).astype(F32)
    gained, scale = (down * gain_ref[...]).astype(BF16), rms(down)
    channel_head = lax.broadcasted_iota(jnp.int32, (1, depth), 1) >> (HD.bit_length() - 1)
    key_head = lax.broadcasted_iota(jnp.int32, (1, heads * rows), 1) >> (rows.bit_length() - 1)
    key_row_head = lax.broadcasted_iota(jnp.int32, (heads * rows, 1), 0) >> (rows.bit_length() - 1)
    spread = jnp.where(key_row_head == channel_head, 1.0, 0.0).astype(BF16)

    def by_head(block):
        wide = block.astype(F32)
        return jnp.concatenate([jnp.where(channel_head == h, wide, 0.0) for h in range(heads)]).astype(BF16)

    def pixel(number):
        return (number & (plan.ncol - 1)) + ((number >> (plan.back.bit_length() - 1)) & (plan.rows - 1)) * plan.ncol

    query_pixel = pixel(lax.broadcasted_iota(jnp.int32, (rows, 1), 0))
    key_pixel = pixel(lax.broadcasted_iota(jnp.int32, (1, heads * rows), 1) & (rows - 1))
    same = query_pixel == key_pixel
    first = lax.axis_index("space") < CORES
    projected = jnp.where(first, 1.0, 0.0) * down
    both = range(CORES)
    qkv = [(dot(gained, qkv_ref[k]) * scale).astype(BF16) for k in both]
    keys = [by_head(qkv[k][:, depth : 2 * depth]) for k in both]
    values = [by_head(qkv[k][:, 2 * depth :]) for k in both]
    scores = [dot_trans(qkv[k][:, :depth], keys[k]) * (HD**-0.5) for k in both]
    weights = []
    for score in scores:
        score = jnp.where(same, score, -jnp.inf)
        top = None
        for h in range(heads):
            peak = jnp.max(jnp.where(key_head == h, score, -jnp.inf), axis=-1, keepdims=True)
            top = peak if h == 0 else jnp.where(key_head >= h, peak, top)
        weights.append(jnp.exp(score - top).astype(BF16))
    mixed = [(dot(w, v) / dot(w, spread)).astype(BF16) for w, v in zip(weights, values)]
    projected = projected + dot(mixed[0], own_out[...]) + dot(mixed[1], other_out[...])
    width = plan.back_width
    parts = [projected[:, k * width : (k + 1) * width] for k in range(plan.lanes)]
    parts = [part.reshape(plan.peers, plan.back, width) for part in parts]
    out_ref[...] = jnp.concatenate(parts, axis=1).reshape(plan.peers * plan.back_rows, width).astype(BF16)


def end_kernel(plan, got_ref, order_ref, latents_ref, out_ref):
    rows = plan.pairs * plan.cols
    bottom = dot(order_ref[...], got_ref[...])
    bottom = jnp.concatenate([bottom[k * rows : (k + 1) * rows] for k in range(plan.lanes)], axis=1)
    bottom = bottom.astype(BF16).astype(F32)
    for f in range(plan.views):
        block = bottom[(f // 2) * plan.cols : (f // 2 + 1) * plan.cols]
        out_ref[f] = (latents_ref[f].astype(F32) + block).astype(BF16)


def call(kernel, name, shapes, args, scratch=(), flops=0, space=pltpu.VMEM):
    outs = [s if isinstance(s, jax.ShapeDtypeStruct) else jax.ShapeDtypeStruct(s, BF16) for s in shapes]
    moved = sum(a.size * a.dtype.itemsize for a in (*args, *outs))
    return pl.pallas_call(
        kernel,
        out_shape=outs,
        in_specs=[pl.BlockSpec(memory_space=space)] * len(args),
        out_specs=[pl.BlockSpec(memory_space=pltpu.VMEM)] * len(outs),
        scratch_shapes=list(scratch),
        compiler_params=pltpu.CompilerParams(vmem_limit_bytes=16 * 2**20),
        cost_estimate=pl.CostEstimate(flops=flops, bytes_accessed=moved, transcendentals=0),
        name=name,
    )(*args)


def body(latents, conv_gain, spatial_weight, temporal_weight, attn_gain, qkv_weight, out_weight):
    views, _, cols, chans = latents.shape
    orbit, space = lax.axis_size("orbit"), lax.axis_size("space")
    plan = Plan(orbit, space, views, cols, chans, spatial_weight.shape[2])
    conv_gain, attn_gain = conv_gain.reshape(1, chans), attn_gain.reshape(1, chans)

    def swap(block, distance):
        return lax.ppermute(block, "space", [(s, s ^ distance) for s in range(space)])

    def exchange(blocks, groups):
        return lax.all_to_all(blocks, ("orbit", "space"), 0, 0, tiled=True, axis_index_groups=groups)

    by_core = [[o * space + x * CORES + c for o in range(orbit) for c in range(CORES)] for x in range(plan.x)]
    by_x = [[o * space + x * CORES + c for o in range(orbit) for x in range(plan.x)] for c in range(CORES)]

    own = latents.reshape(views * cols, chans)
    far = [swap(own, x * CORES) for x in range(1, plan.x)]
    near = swap(own, 1)
    depth, per_row = plan.slice_chans, views * cols
    (taps,) = call(turn_conv_kernel, "turn_conv", [(3, chans, 3 * depth)], (spatial_weight,), flops=60 * 10**9)
    other_temporal, other_out = swap(temporal_weight, 1), swap(out_weight, 1)
    far, near, taps = lax.optimization_barrier((far, near, taps))
    across = [swap(block, 1) for block in far]
    total_shape = (space + 2, per_row, depth)
    (early,) = call(
        functools.partial(early_kernel, plan),
        "conv_early",
        [jax.ShapeDtypeStruct(total_shape, F32)],
        (conv_gain, taps, own, near, *far),
        flops=6 * 10**9,
    )
    count = space * per_row
    (activated,) = call(
        functools.partial(late_kernel, plan),
        "conv_late",
        [(count, depth)],
        (conv_gain, taps, plan.send_order(), early, *across),
        [pltpu.VMEM(total_shape, F32)],
        flops=2 * 9 * count * chans * depth,
    )
    swapped = (other_temporal, other_out)
    activated, swapped, qkv = lax.optimization_barrier((activated, swapped, qkv_weight))
    (other_temporal, other_out), other_qkv = swapped, swap(qkv, 1)
    got = exchange(activated.reshape(orbit * CORES, plan.send_rows, plan.slice_chans), by_core)
    (down,) = call(
        functools.partial(temporal_kernel, plan),
        "temporal",
        [(plan.down_rows, chans)],
        (got.reshape(orbit, CORES, plan.send_rows, plan.slice_chans), temporal_weight, other_temporal),
        flops=2 * 6 * plan.down_rows * chans * plan.slice_chans,
    )
    down, own_qkv, other_qkv = lax.optimization_barrier((down, qkv_weight, other_qkv))
    downs = [down] + [swap(down, x * CORES) for x in range(1, plan.x)]
    (qkv,) = call(
        turn_kernel,
        "turn",
        [(2, chans, 3 * plan.slice_chans)],
        (own_qkv, other_qkv),
        flops=6 * 10**9,
    )
    peers = plan.peers
    (back,) = call(
        functools.partial(attend_kernel, plan),
        "attend",
        [(peers * plan.back_rows, plan.back_width)],
        (attn_gain, qkv, out_weight, other_out, *downs),
        flops=2 * 8 * plan.down_rows * chans * plan.slice_chans,
    )
    got = exchange(back.reshape(peers, plan.back_rows, plan.back_width), None if plan.by_column else by_x)
    (restored,) = call(
        functools.partial(end_kernel, plan),
        "restore",
        [(views, cols, chans)],
        (got.reshape(peers * plan.back_rows, plan.back_width), plan.end_order(), latents.reshape(views, cols, chans)),
    )
    return restored.reshape(latents.shape)


def solution(mesh):
    return jax.shard_map(
        body,
        mesh=mesh,
        in_specs=(
            P("orbit", "space", None, None),
            P(),
            P(None, None, "space", None),
            P(None, "space", None),
            P(),
            P(None, "space", None),
            P("space", None),
        ),
        out_specs=P("orbit", "space", None, None),
        check_vma=False,
    )
```

```python
import functools

import jax
import jax.numpy as jnp
import numpy as np
from jax import lax
from jax.experimental import pallas as pl
from jax.experimental.pallas import tpu as pltpu
from jax.sharding import PartitionSpec as P

HD = 64
CORES = 2
F32 = jnp.float32
BF16 = jnp.bfloat16


def dot(left, right):
    return jnp.dot(left, right, preferred_element_type=F32)


def dot_trans(left, right):
    return lax.dot_general(left, right, (((1,), (1,)), ((), ())), preferred_element_type=F32)


def rms(wide):
    return lax.rsqrt(jnp.mean(wide * wide, axis=-1, keepdims=True) + 1e-06)


def rms_scale(wide, gain):
    return wide * rms(wide) * gain


def picks(source, width):
    return jnp.asarray(np.asarray(source).reshape(-1, 1) == np.arange(width), BF16)


class Plan:
    def __init__(self, orbit, space, views, cols, chans, slice_chans):
        self.orbit, self.space, self.views = orbit, space, views
        self.cols, self.chans, self.slice_chans = cols, chans, slice_chans
        self.x = space // CORES
        share = cols // orbit
        self.by_column = share % CORES == 0
        self.ncol = share // CORES if self.by_column else share
        self.rows = space if self.by_column else self.x
        self.strided = self.by_column and self.ncol == 1 and slice_chans % 128 == 0
        self.pixels = self.rows * self.ncol
        self.pairs = views // 2
        self.down_rows = self.pairs * orbit * self.pixels
        self.send_rows = views * self.pixels
        self.peers = orbit * self.rows
        self.back = self.pairs * self.ncol
        self.lanes = next(n for n in (1, 2, 4, 8) if self.back * n % 8 == 0)
        self.back_rows, self.back_width = self.back * self.lanes, chans // self.lanes

    def column(self, o, core, c):
        return (o * CORES + core) * self.ncol + c if self.by_column else o * self.ncol + c

    def send_order(self):
        o, core, odd, r, pair, c = np.indices((self.orbit, CORES, 2, self.rows, self.pairs, self.ncol))
        row = r if self.by_column else r * CORES + core
        source = (row * self.views + 2 * pair + odd) * self.cols + self.column(o, core, c)
        return picks(source, self.space * self.views * self.cols)

    def end_order(self):
        o, s, lane, view, c = np.indices((self.orbit, self.rows, self.lanes, self.pairs, self.ncol))
        target = (lane * self.pairs + view) * self.cols + self.column(o, s % CORES, c)
        count = self.lanes * self.pairs * self.cols
        return jnp.asarray(target.reshape(1, -1) == np.arange(count).reshape(-1, 1), BF16)


def turn_conv_kernel(weight_ref, out_ref):
    taps, _, depth, chans = weight_ref.shape
    for i in range(taps):
        out_ref[i] = weight_ref[i].reshape(taps * depth, chans).T


def add_rows(plan, blocks, places, weight_ref, total):
    per_row, cols, depth = plan.views * plan.cols, plan.cols, plan.slice_chans
    rows = jnp.concatenate(blocks)
    count = rows.shape[0]
    column = lax.broadcasted_iota(jnp.int32, (count, 1), 0) & (cols - 1)
    for i in range(3):
        part = dot(rows, weight_ref[i])
        left, middle, right = [part[:, j * depth : (j + 1) * depth] for j in range(3)]
        left = jnp.where(column == 0, 0.0, pltpu.roll(left, 1, 0))
        right = jnp.where(column == cols - 1, 0.0, pltpu.roll(right, count - 1, 0))
        part = left + middle + right
        for n, place in enumerate(places):
            start = pl.multiple_of((place + 2 - i) * per_row, per_row)
            total[pl.ds(start, per_row)] += part[n * per_row : (n + 1) * per_row]


def early_kernel(plan, gain_ref, weight_ref, *refs):
    raw_refs, total_ref = refs[:-1], refs[-1]
    gain, space = gain_ref[...], lax.axis_index("space")
    blocks = [rms_scale(ref[...].astype(F32), gain).astype(BF16) for ref in raw_refs]
    places = [space, space ^ 1] + [space ^ (x * CORES) for x in range(1, plan.x)]
    total_ref[...] = jnp.zeros_like(total_ref)
    add_rows(plan, blocks, places, weight_ref, total_ref)


def late_kernel(plan, gain_ref, weight_ref, early_ref, *refs):
    order_refs, raw_refs, (out_ref, total, tiles) = refs[: 1 - plan.strided], refs[1 - plan.strided : -3], refs[-3:]
    gain, space = gain_ref[...], lax.axis_index("space")
    blocks = [rms_scale(ref[...].astype(F32), gain).astype(BF16) for ref in raw_refs]
    places = [space ^ (x * CORES + 1) for x in range(1, plan.x)]
    total[...] = early_ref[...]
    add_rows(plan, blocks, places, weight_ref, total)
    per_row, cols, depth = plan.views * plan.cols, plan.cols, plan.slice_chans
    if plan.strided:
        lanes = [slice(k * 128, (k + 1) * 128) for k in range(depth // 128)]
        for k, lane in enumerate(lanes):
            whole = total[per_row : (plan.space + 1) * per_row, lane]
            tiles[k] = whole / (1.0 + jnp.exp(-whole))
        half = plan.send_rows // 2
        for column in range(cols):
            for k, lane in enumerate(lanes):
                picked = [tiles[k, pl.ds(odd * cols + column, half, stride=2 * cols), :] for odd in range(2)]
                out_ref[column * plan.send_rows : (column + 1) * plan.send_rows, lane] = jnp.concatenate(picked).astype(BF16)
    else:
        whole = total[per_row : (plan.space + 1) * per_row]
        activated = (whole / (1.0 + jnp.exp(-whole))).astype(BF16)
        out_ref[...] = dot(order_refs[0][...], activated).astype(BF16)


def temporal_kernel(plan, got_ref, own_ref, other_ref, out_ref):
    core = lax.rem(lax.axis_index("space"), CORES)
    half, depth = plan.send_rows // 2, plan.slice_chans
    row = lax.broadcasted_iota(jnp.int32, (plan.down_rows, 1), 0)
    first = (row & (plan.back - 1)) < plan.ncol
    total = None
    for index, weight_ref in ((core, own_ref), (1 - core, other_ref)):
        block = got_ref[:, index].astype(F32)
        even = block[:, :half].reshape(plan.down_rows, depth)
        odd = block[:, half:].reshape(plan.down_rows, depth)
        before = jnp.where(first, pltpu.roll(odd, half - plan.back + plan.ncol, 0), pltpu.roll(odd, plan.ncol, 0))
        for k, rows in enumerate((before, even, odd)):
            part = dot(rows.astype(BF16), weight_ref[k])
            total = part if total is None else total + part
    out_ref[...] = total.astype(BF16)


def turn_kernel(own_ref, other_ref, out_ref):
    kinds, depth, chans = own_ref.shape
    for k, ref in enumerate((own_ref, other_ref)):
        out_ref[k] = ref[...].reshape(kinds * depth, chans).T


def attend_kernel(plan, gain_ref, qkv_ref, own_out, other_out, *refs):
    down_refs, out_ref = refs[:-1], refs[-1]
    rows, depth = plan.down_rows, plan.slice_chans
    heads = depth // HD
    down = down_refs[0][...].astype(F32)
    for ref in down_refs[1:]:
        down = down + ref[...].astype(F32)
    down = down.astype(BF16).astype(F32)
    gained, scale = (down * gain_ref[...]).astype(BF16), rms(down)
    channel_head = lax.broadcasted_iota(jnp.int32, (1, depth), 1) >> (HD.bit_length() - 1)
    key_head = lax.broadcasted_iota(jnp.int32, (1, heads * rows), 1) >> (rows.bit_length() - 1)
    key_row_head = lax.broadcasted_iota(jnp.int32, (heads * rows, 1), 0) >> (rows.bit_length() - 1)
    spread = jnp.where(key_row_head == channel_head, 1.0, 0.0).astype(BF16)

    def by_head(block):
        wide = block.astype(F32)
        return jnp.concatenate([jnp.where(channel_head == h, wide, 0.0) for h in range(heads)]).astype(BF16)

    def pixel(number):
        return (number & (plan.ncol - 1)) + ((number >> (plan.back.bit_length() - 1)) & (plan.rows - 1)) * plan.ncol

    query_pixel = pixel(lax.broadcasted_iota(jnp.int32, (rows, 1), 0))
    key_pixel = pixel(lax.broadcasted_iota(jnp.int32, (1, heads * rows), 1) & (rows - 1))
    same = query_pixel == key_pixel
    first = lax.axis_index("space") < CORES
    projected = jnp.where(first, 1.0, 0.0) * down
    both = range(CORES)
    qkv = [(dot(gained, qkv_ref[k]) * scale).astype(BF16) for k in both]
    keys = [by_head(qkv[k][:, depth : 2 * depth]) for k in both]
    values = [by_head(qkv[k][:, 2 * depth :]) for k in both]
    scores = [dot_trans(qkv[k][:, :depth], keys[k]) * (HD**-0.5) for k in both]
    weights = []
    for score in scores:
        score = jnp.where(same, score, -jnp.inf)
        top = None
        for h in range(heads):
            peak = jnp.max(jnp.where(key_head == h, score, -jnp.inf), axis=-1, keepdims=True)
            top = peak if h == 0 else jnp.where(key_head >= h, peak, top)
        weights.append(jnp.exp(score - top).astype(BF16))
    mixed = [(dot(w, v) / dot(w, spread)).astype(BF16) for w, v in zip(weights, values)]
    projected = projected + dot(mixed[0], own_out[...]) + dot(mixed[1], other_out[...])
    width = plan.back_width
    parts = [projected[:, k * width : (k + 1) * width] for k in range(plan.lanes)]
    parts = [part.reshape(plan.peers, plan.back, width) for part in parts]
    out_ref[...] = jnp.concatenate(parts, axis=1).reshape(plan.peers * plan.back_rows, width).astype(BF16)


def end_kernel(plan, got_ref, order_ref, latents_ref, out_ref):
    rows = plan.pairs * plan.cols
    bottom = dot(order_ref[...], got_ref[...])
    bottom = jnp.concatenate([bottom[k * rows : (k + 1) * rows] for k in range(plan.lanes)], axis=1)
    bottom = bottom.astype(BF16).astype(F32)
    for f in range(plan.views):
        block = bottom[(f // 2) * plan.cols : (f // 2 + 1) * plan.cols]
        out_ref[f] = (latents_ref[f].astype(F32) + block).astype(BF16)


def call(kernel, name, shapes, args, scratch=(), flops=0, space=pltpu.VMEM):
    outs = [s if isinstance(s, jax.ShapeDtypeStruct) else jax.ShapeDtypeStruct(s, BF16) for s in shapes]
    moved = sum(a.size * a.dtype.itemsize for a in (*args, *outs))
    return pl.pallas_call(
        kernel,
        out_shape=outs,
        in_specs=[pl.BlockSpec(memory_space=space)] * len(args),
        out_specs=[pl.BlockSpec(memory_space=pltpu.VMEM)] * len(outs),
        scratch_shapes=list(scratch),
        compiler_params=pltpu.CompilerParams(vmem_limit_bytes=16 * 2**20),
        cost_estimate=pl.CostEstimate(flops=flops, bytes_accessed=moved, transcendentals=0),
        name=name,
    )(*args)


def body(latents, conv_gain, spatial_weight, temporal_weight, attn_gain, qkv_weight, out_weight):
    views, _, cols, chans = latents.shape
    orbit, space = lax.axis_size("orbit"), lax.axis_size("space")
    plan = Plan(orbit, space, views, cols, chans, spatial_weight.shape[2])
    conv_gain, attn_gain = conv_gain.reshape(1, chans), attn_gain.reshape(1, chans)

    def swap(block, distance):
        return lax.ppermute(block, "space", [(s, s ^ distance) for s in range(space)])

    def exchange(blocks, groups):
        return lax.all_to_all(blocks, ("orbit", "space"), 0, 0, tiled=True, axis_index_groups=groups)

    by_core = [[o * space + x * CORES + c for o in range(orbit) for c in range(CORES)] for x in range(plan.x)]
    by_x = [[o * space + x * CORES + c for o in range(orbit) for x in range(plan.x)] for c in range(CORES)]

    own = latents.reshape(views * cols, chans)
    far = [swap(own, x * CORES) for x in range(1, plan.x)]
    near = swap(own, 1)
    depth, per_row = plan.slice_chans, views * cols
    (taps,) = call(turn_conv_kernel, "turn_conv", [(3, chans, 3 * depth)], (spatial_weight,), flops=60 * 10**9)
    other_temporal, other_out = swap(temporal_weight, 1), swap(out_weight, 1)
    far, near, taps = lax.optimization_barrier((far, near, taps))
    across = [swap(block, 1) for block in far]
    total_shape = ((space + 2) * per_row, depth)
    order = [] if plan.strided else [plan.send_order()]
    (early,) = call(
        functools.partial(early_kernel, plan),
        "conv_early",
        [jax.ShapeDtypeStruct(total_shape, F32)],
        (conv_gain, taps, own, near, *far),
        flops=6 * 10**9,
    )
    count = space * per_row
    (activated,) = call(
        functools.partial(late_kernel, plan),
        "conv_late",
        [(count, depth)],
        (conv_gain, taps, early, *order, *across),
        [pltpu.VMEM(total_shape, F32), pltpu.VMEM((max(depth // 128, 1), count, 128), F32)],
        flops=2 * 9 * count * chans * depth,
    )
    swapped = (other_temporal, other_out)
    activated, swapped, qkv = lax.optimization_barrier((activated, swapped, qkv_weight))
    (other_temporal, other_out), other_qkv = swapped, swap(qkv, 1)
    got = exchange(activated.reshape(orbit * CORES, plan.send_rows, plan.slice_chans), by_core)
    (down,) = call(
        functools.partial(temporal_kernel, plan),
        "temporal",
        [(plan.down_rows, chans)],
        (got.reshape(orbit, CORES, plan.send_rows, plan.slice_chans), temporal_weight, other_temporal),
        flops=2 * 6 * plan.down_rows * chans * plan.slice_chans,
    )
    down, own_qkv, other_qkv = lax.optimization_barrier((down, qkv_weight, other_qkv))
    downs = [down] + [swap(down, x * CORES) for x in range(1, plan.x)]
    (qkv,) = call(
        turn_kernel,
        "turn",
        [(2, chans, 3 * plan.slice_chans)],
        (own_qkv, other_qkv),
        flops=6 * 10**9,
    )
    peers = plan.peers
    (back,) = call(
        functools.partial(attend_kernel, plan),
        "attend",
        [(peers * plan.back_rows, plan.back_width)],
        (attn_gain, qkv, out_weight, other_out, *downs),
        flops=2 * 8 * plan.down_rows * chans * plan.slice_chans,
    )
    got = exchange(back.reshape(peers, plan.back_rows, plan.back_width), None if plan.by_column else by_x)
    (restored,) = call(
        functools.partial(end_kernel, plan),
        "restore",
        [(views, cols, chans)],
        (got.reshape(peers * plan.back_rows, plan.back_width), plan.end_order(), latents.reshape(views, cols, chans)),
    )
    return restored.reshape(latents.shape)


def solution(mesh):
    return jax.shard_map(
        body,
        mesh=mesh,
        in_specs=(
            P("orbit", "space", None, None),
            P(),
            P(None, None, "space", None),
            P(None, "space", None),
            P(),
            P(None, "space", None),
            P("space", None),
        ),
        out_specs=P("orbit", "space", None, None),
        check_vma=False,
    )
```

```python
import functools

import jax
import jax.numpy as jnp
import numpy as np
from jax import lax
from jax.experimental import pallas as pl
from jax.experimental.pallas import tpu as pltpu
from jax.sharding import PartitionSpec as P

HD = 64
CORES = 2
F32 = jnp.float32
BF16 = jnp.bfloat16


def dot(left, right):
    return jnp.dot(left, right, preferred_element_type=F32)


def dot_trans(left, right):
    return lax.dot_general(left, right, (((1,), (1,)), ((), ())), preferred_element_type=F32)


def rms(wide):
    return lax.rsqrt(jnp.mean(wide * wide, axis=-1, keepdims=True) + 1e-06)


def rms_scale(wide, gain):
    return wide * rms(wide) * gain


def picks(source, width):
    return jnp.asarray(np.asarray(source).reshape(-1, 1) == np.arange(width), BF16)


class Plan:
    def __init__(self, orbit, space, views, cols, chans, slice_chans):
        self.orbit, self.space, self.views = orbit, space, views
        self.cols, self.chans, self.slice_chans = cols, chans, slice_chans
        self.x = space // CORES
        share = cols // orbit
        self.by_column = share % CORES == 0
        self.ncol = share // CORES if self.by_column else share
        self.rows = space if self.by_column else self.x
        self.strided = self.by_column and self.ncol == 1 and slice_chans % 128 == 0
        self.pixels = self.rows * self.ncol
        self.pairs = views // 2
        self.down_rows = self.pairs * orbit * self.pixels
        self.send_rows = views * self.pixels
        self.peers = orbit * self.rows
        self.back = self.pairs * self.ncol
        self.lanes = next(n for n in (1, 2, 4, 8) if self.back * n % 8 == 0)
        self.back_rows, self.back_width = self.back * self.lanes, chans // self.lanes

    def column(self, o, core, c):
        return (o * CORES + core) * self.ncol + c if self.by_column else o * self.ncol + c

    def send_order(self):
        o, core, odd, r, pair, c = np.indices((self.orbit, CORES, 2, self.rows, self.pairs, self.ncol))
        row = r if self.by_column else r * CORES + core
        source = (row * self.views + 2 * pair + odd) * self.cols + self.column(o, core, c)
        return picks(source, self.space * self.views * self.cols)

    def end_order(self):
        o, s, lane, view, c = np.indices((self.orbit, self.rows, self.lanes, self.pairs, self.ncol))
        target = (lane * self.pairs + view) * self.cols + self.column(o, s % CORES, c)
        count = self.lanes * self.pairs * self.cols
        return jnp.asarray(target.reshape(1, -1) == np.arange(count).reshape(-1, 1), BF16)


def turn_conv_kernel(weight_ref, out_ref):
    taps, _, depth, chans = weight_ref.shape
    for i in range(taps):
        out_ref[i] = weight_ref[i].reshape(taps * depth, chans).T


def add_rows(plan, blocks, places, weight_ref, total):
    per_row, cols, depth = plan.views * plan.cols, plan.cols, plan.slice_chans
    rows = jnp.concatenate(blocks)
    count = rows.shape[0]
    column = lax.broadcasted_iota(jnp.int32, (count, 1), 0) & (cols - 1)
    for i in range(3):
        part = dot(rows, weight_ref[i])
        left, middle, right = [part[:, j * depth : (j + 1) * depth] for j in range(3)]
        left = jnp.where(column == 0, 0.0, pltpu.roll(left, 1, 0))
        right = jnp.where(column == cols - 1, 0.0, pltpu.roll(right, count - 1, 0))
        part = left + middle + right
        for n, place in enumerate(places):
            start = pl.multiple_of((place + 2 - i) * per_row, per_row)
            total[pl.ds(start, per_row)] += part[n * per_row : (n + 1) * per_row]


def early_kernel(plan, gain_ref, weight_ref, *refs):
    raw_refs, total_ref = refs[:-1], refs[-1]
    gain, space = gain_ref[...], lax.axis_index("space")
    blocks = [rms_scale(ref[...].astype(F32), gain).astype(BF16) for ref in raw_refs]
    places = [space, space ^ 1] + [space ^ (x * CORES) for x in range(1, plan.x)]
    total_ref[...] = jnp.zeros_like(total_ref)
    add_rows(plan, blocks, places, weight_ref, total_ref)


def late_kernel(plan, gain_ref, weight_ref, early_ref, *refs):
    order_refs, raw_refs, (out_ref, total, tiles) = refs[: 1 - plan.strided], refs[1 - plan.strided : -3], refs[-3:]
    gain, space = gain_ref[...], lax.axis_index("space")
    blocks = [rms_scale(ref[...].astype(F32), gain).astype(BF16) for ref in raw_refs]
    places = [space ^ (x * CORES + 1) for x in range(1, plan.x)]
    total[...] = early_ref[...]
    add_rows(plan, blocks, places, weight_ref, total)
    per_row, cols, depth = plan.views * plan.cols, plan.cols, plan.slice_chans
    if plan.strided:
        lanes = [slice(k * 128, (k + 1) * 128) for k in range(depth // 128)]
        for k, lane in enumerate(lanes):
            whole = total[per_row : (plan.space + 1) * per_row, lane]
            tiles[k] = whole / (1.0 + jnp.exp(-whole))
        half = plan.send_rows // 2
        for column in range(cols):
            for k, lane in enumerate(lanes):
                picked = [tiles[k, pl.ds(odd * cols + column, half, stride=2 * cols), :] for odd in range(2)]
                out_ref[column * plan.send_rows : (column + 1) * plan.send_rows, lane] = jnp.concatenate(picked).astype(BF16)
    else:
        whole = total[per_row : (plan.space + 1) * per_row]
        activated = (whole / (1.0 + jnp.exp(-whole))).astype(BF16)
        out_ref[...] = dot(order_refs[0][...], activated).astype(BF16)


def temporal_kernel(plan, got_ref, own_ref, other_ref, out_ref):
    core = lax.rem(lax.axis_index("space"), CORES)
    half, depth = plan.send_rows // 2, plan.slice_chans
    row = lax.broadcasted_iota(jnp.int32, (plan.down_rows, 1), 0)
    first = (row & (plan.back - 1)) < plan.ncol
    lefts, rights = [], []
    for index, weight_ref in ((core, own_ref), (1 - core, other_ref)):
        block = got_ref[:, index].astype(F32)
        even = block[:, :half].reshape(plan.down_rows, depth)
        odd = block[:, half:].reshape(plan.down_rows, depth)
        before = jnp.where(first, pltpu.roll(odd, half - plan.back + plan.ncol, 0), pltpu.roll(odd, plan.ncol, 0))
        lefts += [before.astype(BF16), even.astype(BF16), odd.astype(BF16)]
        rights.append(weight_ref[...].reshape(3 * depth, plan.chans))
    out_ref[...] = dot(jnp.concatenate(lefts, axis=1), jnp.concatenate(rights)).astype(BF16)


def turn_kernel(own_ref, other_ref, out_ref):
    kinds, depth, chans = own_ref.shape
    for k, ref in enumerate((own_ref, other_ref)):
        out_ref[k] = ref[...].reshape(kinds * depth, chans).T


def attend_kernel(plan, gain_ref, qkv_ref, own_out, other_out, *refs):
    down_refs, out_ref = refs[:-1], refs[-1]
    rows, depth = plan.down_rows, plan.slice_chans
    heads = depth // HD
    down = down_refs[0][...].astype(F32)
    for ref in down_refs[1:]:
        down = down + ref[...].astype(F32)
    down = down.astype(BF16).astype(F32)
    gained, scale = (down * gain_ref[...]).astype(BF16), rms(down)
    channel_head = lax.broadcasted_iota(jnp.int32, (1, depth), 1) >> (HD.bit_length() - 1)
    key_head = lax.broadcasted_iota(jnp.int32, (1, heads * rows), 1) >> (rows.bit_length() - 1)
    key_row_head = lax.broadcasted_iota(jnp.int32, (heads * rows, 1), 0) >> (rows.bit_length() - 1)
    spread = jnp.where(key_row_head == channel_head, 1.0, 0.0).astype(BF16)

    def by_head(block):
        wide = block.astype(F32)
        return jnp.concatenate([jnp.where(channel_head == h, wide, 0.0) for h in range(heads)]).astype(BF16)

    def pixel(number):
        return (number & (plan.ncol - 1)) + ((number >> (plan.back.bit_length() - 1)) & (plan.rows - 1)) * plan.ncol

    query_pixel = pixel(lax.broadcasted_iota(jnp.int32, (rows, 1), 0))
    key_pixel = pixel(lax.broadcasted_iota(jnp.int32, (1, heads * rows), 1) & (rows - 1))
    same = query_pixel == key_pixel
    first = lax.axis_index("space") < CORES
    projected = jnp.where(first, 1.0, 0.0) * down
    both = range(CORES)
    qkv = [(dot(gained, qkv_ref[k]) * scale).astype(BF16) for k in both]
    keys = [by_head(qkv[k][:, depth : 2 * depth]) for k in both]
    values = [by_head(qkv[k][:, 2 * depth :]) for k in both]
    scores = [dot_trans(qkv[k][:, :depth], keys[k]) * (HD**-0.5) for k in both]
    weights = []
    for score in scores:
        score = jnp.where(same, score, -jnp.inf)
        top = None
        for h in range(heads):
            peak = jnp.max(jnp.where(key_head == h, score, -jnp.inf), axis=-1, keepdims=True)
            top = peak if h == 0 else jnp.where(key_head >= h, peak, top)
        weights.append(jnp.exp(score - top).astype(BF16))
    mixed = [(dot(w, v) / dot(w, spread)).astype(BF16) for w, v in zip(weights, values)]
    projected = projected + dot(mixed[0], own_out[...]) + dot(mixed[1], other_out[...])
    width = plan.back_width
    parts = [projected[:, k * width : (k + 1) * width] for k in range(plan.lanes)]
    parts = [part.reshape(plan.peers, plan.back, width) for part in parts]
    out_ref[...] = jnp.concatenate(parts, axis=1).reshape(plan.peers * plan.back_rows, width).astype(BF16)


def end_kernel(plan, got_ref, order_ref, latents_ref, out_ref):
    rows = plan.pairs * plan.cols
    bottom = dot(order_ref[...], got_ref[...])
    bottom = jnp.concatenate([bottom[k * rows : (k + 1) * rows] for k in range(plan.lanes)], axis=1)
    bottom = bottom.astype(BF16).astype(F32)
    for f in range(plan.views):
        block = bottom[(f // 2) * plan.cols : (f // 2 + 1) * plan.cols]
        out_ref[f] = (latents_ref[f].astype(F32) + block).astype(BF16)


def call(kernel, name, shapes, args, scratch=(), flops=0, space=pltpu.VMEM):
    outs = [s if isinstance(s, jax.ShapeDtypeStruct) else jax.ShapeDtypeStruct(s, BF16) for s in shapes]
    moved = sum(a.size * a.dtype.itemsize for a in (*args, *outs))
    return pl.pallas_call(
        kernel,
        out_shape=outs,
        in_specs=[pl.BlockSpec(memory_space=space)] * len(args),
        out_specs=[pl.BlockSpec(memory_space=pltpu.VMEM)] * len(outs),
        scratch_shapes=list(scratch),
        compiler_params=pltpu.CompilerParams(vmem_limit_bytes=16 * 2**20),
        cost_estimate=pl.CostEstimate(flops=flops, bytes_accessed=moved, transcendentals=0),
        name=name,
    )(*args)


def body(latents, conv_gain, spatial_weight, temporal_weight, attn_gain, qkv_weight, out_weight):
    views, _, cols, chans = latents.shape
    orbit, space = lax.axis_size("orbit"), lax.axis_size("space")
    plan = Plan(orbit, space, views, cols, chans, spatial_weight.shape[2])
    conv_gain, attn_gain = conv_gain.reshape(1, chans), attn_gain.reshape(1, chans)

    def swap(block, distance):
        return lax.ppermute(block, "space", [(s, s ^ distance) for s in range(space)])

    def exchange(blocks, groups):
        return lax.all_to_all(blocks, ("orbit", "space"), 0, 0, tiled=True, axis_index_groups=groups)

    by_core = [[o * space + x * CORES + c for o in range(orbit) for c in range(CORES)] for x in range(plan.x)]
    by_x = [[o * space + x * CORES + c for o in range(orbit) for x in range(plan.x)] for c in range(CORES)]

    own = latents.reshape(views * cols, chans)
    far = [swap(own, x * CORES) for x in range(1, plan.x)]
    near = swap(own, 1)
    depth, per_row = plan.slice_chans, views * cols
    (taps,) = call(turn_conv_kernel, "turn_conv", [(3, chans, 3 * depth)], (spatial_weight,), flops=60 * 10**9)
    other_temporal, other_out = swap(temporal_weight, 1), swap(out_weight, 1)
    far, near, taps = lax.optimization_barrier((far, near, taps))
    across = [swap(block, 1) for block in far]
    total_shape = ((space + 2) * per_row, depth)
    order = [] if plan.strided else [plan.send_order()]
    (early,) = call(
        functools.partial(early_kernel, plan),
        "conv_early",
        [jax.ShapeDtypeStruct(total_shape, F32)],
        (conv_gain, taps, own, near, *far),
        flops=6 * 10**9,
    )
    count = space * per_row
    (activated,) = call(
        functools.partial(late_kernel, plan),
        "conv_late",
        [(count, depth)],
        (conv_gain, taps, early, *order, *across),
        [pltpu.VMEM(total_shape, F32), pltpu.VMEM((max(depth // 128, 1), count, 128), F32)],
        flops=2 * 9 * count * chans * depth,
    )
    swapped = (other_temporal, other_out)
    activated, swapped, qkv = lax.optimization_barrier((activated, swapped, qkv_weight))
    (other_temporal, other_out), other_qkv = swapped, swap(qkv, 1)
    got = exchange(activated.reshape(orbit * CORES, plan.send_rows, plan.slice_chans), by_core)
    (down,) = call(
        functools.partial(temporal_kernel, plan),
        "temporal",
        [(plan.down_rows, chans)],
        (got.reshape(orbit, CORES, plan.send_rows, plan.slice_chans), temporal_weight, other_temporal),
        flops=2 * 6 * plan.down_rows * chans * plan.slice_chans,
    )
    down, own_qkv, other_qkv = lax.optimization_barrier((down, qkv_weight, other_qkv))
    downs = [down] + [swap(down, x * CORES) for x in range(1, plan.x)]
    (qkv,) = call(
        turn_kernel,
        "turn",
        [(2, chans, 3 * plan.slice_chans)],
        (own_qkv, other_qkv),
        flops=6 * 10**9,
    )
    peers = plan.peers
    (back,) = call(
        functools.partial(attend_kernel, plan),
        "attend",
        [(peers * plan.back_rows, plan.back_width)],
        (attn_gain, qkv, out_weight, other_out, *downs),
        flops=2 * 8 * plan.down_rows * chans * plan.slice_chans,
    )
    got = exchange(back.reshape(peers, plan.back_rows, plan.back_width), None if plan.by_column else by_x)
    (restored,) = call(
        functools.partial(end_kernel, plan),
        "restore",
        [(views, cols, chans)],
        (got.reshape(peers * plan.back_rows, plan.back_width), plan.end_order(), latents.reshape(views, cols, chans)),
    )
    return restored.reshape(latents.shape)


def solution(mesh):
    return jax.shard_map(
        body,
        mesh=mesh,
        in_specs=(
            P("orbit", "space", None, None),
            P(),
            P(None, None, "space", None),
            P(None, "space", None),
            P(),
            P(None, "space", None),
            P("space", None),
        ),
        out_specs=P("orbit", "space", None, None),
        check_vma=False,
    )
```

```python
import functools

import jax
import jax.numpy as jnp
import numpy as np
from jax import lax
from jax.experimental import pallas as pl
from jax.experimental.pallas import tpu as pltpu
from jax.sharding import PartitionSpec as P

HD = 64
CORES = 2
F32 = jnp.float32
BF16 = jnp.bfloat16


def dot(left, right):
    return jnp.dot(left, right, preferred_element_type=F32)


def dot_trans(left, right):
    return lax.dot_general(left, right, (((1,), (1,)), ((), ())), preferred_element_type=F32)


def rms(wide):
    return lax.rsqrt(jnp.mean(wide * wide, axis=-1, keepdims=True) + 1e-06)


def rms_scale(wide, gain):
    return wide * rms(wide) * gain


def picks(source, width):
    return jnp.asarray(np.asarray(source).reshape(-1, 1) == np.arange(width), BF16)


class Plan:
    def __init__(self, orbit, space, views, cols, chans, slice_chans):
        self.orbit, self.space, self.views = orbit, space, views
        self.cols, self.chans, self.slice_chans = cols, chans, slice_chans
        self.x = space // CORES
        share = cols // orbit
        self.by_column = share % CORES == 0
        self.ncol = share // CORES if self.by_column else share
        self.rows = space if self.by_column else self.x
        self.strided = self.by_column and self.ncol == 1 and slice_chans % 128 == 0
        self.pixels = self.rows * self.ncol
        self.pairs = views // 2
        self.down_rows = self.pairs * orbit * self.pixels
        self.send_rows = views * self.pixels
        self.peers = orbit * self.rows
        self.back = self.pairs * self.ncol
        self.lanes = next(n for n in (1, 2, 4, 8) if self.back * n % 8 == 0)
        self.back_rows, self.back_width = self.back * self.lanes, chans // self.lanes

    def column(self, o, core, c):
        return (o * CORES + core) * self.ncol + c if self.by_column else o * self.ncol + c

    def send_order(self):
        o, core, odd, r, pair, c = np.indices((self.orbit, CORES, 2, self.rows, self.pairs, self.ncol))
        row = r if self.by_column else r * CORES + core
        source = (row * self.views + 2 * pair + odd) * self.cols + self.column(o, core, c)
        return picks(source, self.space * self.views * self.cols)

    def end_order(self):
        o, s, lane, view, c = np.indices((self.orbit, self.rows, self.lanes, self.pairs, self.ncol))
        target = (lane * self.pairs + view) * self.cols + self.column(o, s % CORES, c)
        count = self.lanes * self.pairs * self.cols
        return jnp.asarray(target.reshape(1, -1) == np.arange(count).reshape(-1, 1), BF16)


def turn_conv_kernel(weight_ref, out_ref):
    taps, _, depth, chans = weight_ref.shape
    for i in range(taps):
        out_ref[i] = weight_ref[i].reshape(taps * depth, chans).T


def add_rows(plan, blocks, places, weight_ref, total):
    per_row, cols, depth = plan.views * plan.cols, plan.cols, plan.slice_chans
    rows = jnp.concatenate(blocks)
    count = rows.shape[0]
    column = lax.broadcasted_iota(jnp.int32, (count, 1), 0) & (cols - 1)
    for i in range(3):
        part = dot(rows, weight_ref[i])
        left, middle, right = [part[:, j * depth : (j + 1) * depth] for j in range(3)]
        left = jnp.where(column == 0, 0.0, pltpu.roll(left, 1, 0))
        right = jnp.where(column == cols - 1, 0.0, pltpu.roll(right, count - 1, 0))
        part = left + middle + right
        for n, place in enumerate(places):
            start = pl.multiple_of((place + 2 - i) * per_row, per_row)
            total[pl.ds(start, per_row)] += part[n * per_row : (n + 1) * per_row]


def early_kernel(plan, gain_ref, weight_ref, *refs):
    raw_refs, total_ref = refs[:-1], refs[-1]
    gain, space = gain_ref[...], lax.axis_index("space")
    blocks = [rms_scale(ref[...].astype(F32), gain).astype(BF16) for ref in raw_refs]
    places = [space, space ^ 1] + [space ^ (x * CORES) for x in range(1, plan.x)]
    total_ref[...] = jnp.zeros_like(total_ref)
    add_rows(plan, blocks, places, weight_ref, total_ref)


def late_kernel(plan, gain_ref, weight_ref, early_ref, *refs):
    order_refs, raw_refs, (out_ref, total, tiles) = refs[: 1 - plan.strided], refs[1 - plan.strided : -3], refs[-3:]
    gain, space = gain_ref[...], lax.axis_index("space")
    blocks = [rms_scale(ref[...].astype(F32), gain).astype(BF16) for ref in raw_refs]
    places = [space ^ (x * CORES + 1) for x in range(1, plan.x)]
    total[...] = early_ref[...]
    add_rows(plan, blocks, places, weight_ref, total)
    per_row, cols, depth = plan.views * plan.cols, plan.cols, plan.slice_chans
    if plan.strided:
        lanes = [slice(k * 128, (k + 1) * 128) for k in range(depth // 128)]
        for k, lane in enumerate(lanes):
            whole = total[per_row : (plan.space + 1) * per_row, lane]
            tiles[k] = whole / (1.0 + jnp.exp(-whole))
        half = plan.send_rows // 2
        for column in range(cols):
            for k, lane in enumerate(lanes):
                picked = [tiles[k, pl.ds(odd * cols + column, half, stride=2 * cols), :] for odd in range(2)]
                out_ref[column * plan.send_rows : (column + 1) * plan.send_rows, lane] = jnp.concatenate(picked).astype(BF16)
    else:
        whole = total[per_row : (plan.space + 1) * per_row]
        activated = (whole / (1.0 + jnp.exp(-whole))).astype(BF16)
        out_ref[...] = dot(order_refs[0][...], activated).astype(BF16)


def temporal_kernel(plan, got_ref, own_ref, other_ref, out_ref):
    core = lax.rem(lax.axis_index("space"), CORES)
    half, depth = plan.send_rows // 2, plan.slice_chans
    row = lax.broadcasted_iota(jnp.int32, (plan.down_rows, 1), 0)
    first = (row & (plan.back - 1)) < plan.ncol
    lefts, rights = [], []
    for index, weight_ref in ((core, own_ref), (1 - core, other_ref)):
        block = got_ref[:, index].astype(F32)
        even = block[:, :half].reshape(plan.down_rows, depth)
        odd = block[:, half:].reshape(plan.down_rows, depth)
        before = jnp.where(first, pltpu.roll(odd, half - plan.back + plan.ncol, 0), pltpu.roll(odd, plan.ncol, 0))
        lefts += [before.astype(BF16), even.astype(BF16), odd.astype(BF16)]
        rights.append(weight_ref[...].reshape(3 * depth, plan.chans))
    out_ref[...] = dot(jnp.concatenate(lefts, axis=1), jnp.concatenate(rights)).astype(BF16)


def turn_kernel(own_ref, other_ref, out_ref):
    kinds, depth, chans = own_ref.shape
    for k, ref in enumerate((own_ref, other_ref)):
        out_ref[k] = ref[...].reshape(kinds * depth, chans).T


def attend_kernel(plan, gain_ref, qkv_ref, own_out, other_out, *refs):
    down_refs, out_ref = refs[:-1], refs[-1]
    rows, depth = plan.down_rows, plan.slice_chans
    heads = depth // HD
    down = down_refs[0][...].astype(F32)
    for ref in down_refs[1:]:
        down = down + ref[...].astype(F32)
    down = down.astype(BF16).astype(F32)
    gained, scale = (down * gain_ref[...]).astype(BF16), rms(down)
    channel_head = lax.broadcasted_iota(jnp.int32, (1, depth), 1) >> (HD.bit_length() - 1)
    key_head = lax.broadcasted_iota(jnp.int32, (1, heads * rows), 1) >> (rows.bit_length() - 1)
    key_row_head = lax.broadcasted_iota(jnp.int32, (heads * rows, 1), 0) >> (rows.bit_length() - 1)
    spread = jnp.where(key_row_head == channel_head, 1.0, 0.0).astype(BF16)

    def by_head(block):
        wide = block.astype(F32)
        return jnp.concatenate([jnp.where(channel_head == h, wide, 0.0) for h in range(heads)]).astype(BF16)

    def pixel(number):
        return (number & (plan.ncol - 1)) + ((number >> (plan.back.bit_length() - 1)) & (plan.rows - 1)) * plan.ncol

    query_pixel = pixel(lax.broadcasted_iota(jnp.int32, (rows, 1), 0))
    key_pixel = pixel(lax.broadcasted_iota(jnp.int32, (1, heads * rows), 1) & (rows - 1))
    same = query_pixel == key_pixel
    first = lax.axis_index("space") < CORES
    projected = jnp.where(first, 1.0, 0.0) * down
    both = range(CORES)
    qkv = [(dot(gained, qkv_ref[k]) * scale).astype(BF16) for k in both]
    keys = [by_head(qkv[k][:, depth : 2 * depth]) for k in both]
    values = [by_head(qkv[k][:, 2 * depth :]) for k in both]
    scores = [dot_trans(qkv[k][:, :depth], keys[k]) * (HD**-0.5) for k in both]
    weights = []
    for score in scores:
        score = jnp.where(same, score, -jnp.inf)
        top = None
        for h in range(heads):
            peak = jnp.max(jnp.where(key_head == h, score, -jnp.inf), axis=-1, keepdims=True)
            top = peak if h == 0 else jnp.where(key_head >= h, peak, top)
        weights.append(jnp.exp(score - top).astype(BF16))
    mixed = [(dot(w, v) / dot(w, spread)).astype(BF16) for w, v in zip(weights, values)]
    weight = jnp.concatenate([own_out[...], other_out[...]])
    projected = projected + dot(jnp.concatenate(mixed, axis=1), weight)
    width = plan.back_width
    parts = [projected[:, k * width : (k + 1) * width] for k in range(plan.lanes)]
    parts = [part.reshape(plan.peers, plan.back, width) for part in parts]
    out_ref[...] = jnp.concatenate(parts, axis=1).reshape(plan.peers * plan.back_rows, width).astype(BF16)


def end_kernel(plan, got_ref, order_ref, latents_ref, out_ref):
    rows = plan.pairs * plan.cols
    bottom = dot(order_ref[...], got_ref[...])
    bottom = jnp.concatenate([bottom[k * rows : (k + 1) * rows] for k in range(plan.lanes)], axis=1)
    bottom = bottom.astype(BF16).astype(F32)
    for f in range(plan.views):
        block = bottom[(f // 2) * plan.cols : (f // 2 + 1) * plan.cols]
        out_ref[f] = (latents_ref[f].astype(F32) + block).astype(BF16)


def call(kernel, name, shapes, args, scratch=(), flops=0, space=pltpu.VMEM):
    outs = [s if isinstance(s, jax.ShapeDtypeStruct) else jax.ShapeDtypeStruct(s, BF16) for s in shapes]
    moved = sum(a.size * a.dtype.itemsize for a in (*args, *outs))
    return pl.pallas_call(
        kernel,
        out_shape=outs,
        in_specs=[pl.BlockSpec(memory_space=space)] * len(args),
        out_specs=[pl.BlockSpec(memory_space=pltpu.VMEM)] * len(outs),
        scratch_shapes=list(scratch),
        compiler_params=pltpu.CompilerParams(vmem_limit_bytes=16 * 2**20),
        cost_estimate=pl.CostEstimate(flops=flops, bytes_accessed=moved, transcendentals=0),
        name=name,
    )(*args)


def body(latents, conv_gain, spatial_weight, temporal_weight, attn_gain, qkv_weight, out_weight):
    views, _, cols, chans = latents.shape
    orbit, space = lax.axis_size("orbit"), lax.axis_size("space")
    plan = Plan(orbit, space, views, cols, chans, spatial_weight.shape[2])
    conv_gain, attn_gain = conv_gain.reshape(1, chans), attn_gain.reshape(1, chans)

    def swap(block, distance):
        return lax.ppermute(block, "space", [(s, s ^ distance) for s in range(space)])

    def exchange(blocks, groups):
        return lax.all_to_all(blocks, ("orbit", "space"), 0, 0, tiled=True, axis_index_groups=groups)

    by_core = [[o * space + x * CORES + c for o in range(orbit) for c in range(CORES)] for x in range(plan.x)]
    by_x = [[o * space + x * CORES + c for o in range(orbit) for x in range(plan.x)] for c in range(CORES)]

    own = latents.reshape(views * cols, chans)
    far = [swap(own, x * CORES) for x in range(1, plan.x)]
    near = swap(own, 1)
    depth, per_row = plan.slice_chans, views * cols
    (taps,) = call(turn_conv_kernel, "turn_conv", [(3, chans, 3 * depth)], (spatial_weight,), flops=60 * 10**9)
    other_temporal, other_out = swap(temporal_weight, 1), swap(out_weight, 1)
    far, near, taps = lax.optimization_barrier((far, near, taps))
    across = [swap(block, 1) for block in far]
    total_shape = ((space + 2) * per_row, depth)
    order = [] if plan.strided else [plan.send_order()]
    (early,) = call(
        functools.partial(early_kernel, plan),
        "conv_early",
        [jax.ShapeDtypeStruct(total_shape, F32)],
        (conv_gain, taps, own, near, *far),
        flops=6 * 10**9,
    )
    count = space * per_row
    (activated,) = call(
        functools.partial(late_kernel, plan),
        "conv_late",
        [(count, depth)],
        (conv_gain, taps, early, *order, *across),
        [pltpu.VMEM(total_shape, F32), pltpu.VMEM((max(depth // 128, 1), count, 128), F32)],
        flops=2 * 9 * count * chans * depth,
    )
    swapped = (other_temporal, other_out)
    activated, swapped, qkv = lax.optimization_barrier((activated, swapped, qkv_weight))
    (other_temporal, other_out), other_qkv = swapped, swap(qkv, 1)
    got = exchange(activated.reshape(orbit * CORES, plan.send_rows, plan.slice_chans), by_core)
    (down,) = call(
        functools.partial(temporal_kernel, plan),
        "temporal",
        [(plan.down_rows, chans)],
        (got.reshape(orbit, CORES, plan.send_rows, plan.slice_chans), temporal_weight, other_temporal),
        flops=2 * 6 * plan.down_rows * chans * plan.slice_chans,
    )
    down, own_qkv, other_qkv = lax.optimization_barrier((down, qkv_weight, other_qkv))
    downs = [down] + [swap(down, x * CORES) for x in range(1, plan.x)]
    (qkv,) = call(
        turn_kernel,
        "turn",
        [(2, chans, 3 * plan.slice_chans)],
        (own_qkv, other_qkv),
        flops=6 * 10**9,
    )
    peers = plan.peers
    (back,) = call(
        functools.partial(attend_kernel, plan),
        "attend",
        [(peers * plan.back_rows, plan.back_width)],
        (attn_gain, qkv, out_weight, other_out, *downs),
        flops=2 * 8 * plan.down_rows * chans * plan.slice_chans,
    )
    got = exchange(back.reshape(peers, plan.back_rows, plan.back_width), None if plan.by_column else by_x)
    (restored,) = call(
        functools.partial(end_kernel, plan),
        "restore",
        [(views, cols, chans)],
        (got.reshape(peers * plan.back_rows, plan.back_width), plan.end_order(), latents.reshape(views, cols, chans)),
    )
    return restored.reshape(latents.shape)


def solution(mesh):
    return jax.shard_map(
        body,
        mesh=mesh,
        in_specs=(
            P("orbit", "space", None, None),
            P(),
            P(None, None, "space", None),
            P(None, "space", None),
            P(),
            P(None, "space", None),
            P("space", None),
        ),
        out_specs=P("orbit", "space", None, None),
        check_vma=False,
    )
```

```python
import functools

import jax
import jax.numpy as jnp
import numpy as np
from jax import lax
from jax.experimental import pallas as pl
from jax.experimental.pallas import tpu as pltpu
from jax.sharding import PartitionSpec as P

HD = 64
CORES = 2
F32 = jnp.float32
BF16 = jnp.bfloat16


def dot(left, right):
    return jnp.dot(left, right, preferred_element_type=F32)


def dot_trans(left, right):
    return lax.dot_general(left, right, (((1,), (1,)), ((), ())), preferred_element_type=F32)


def rms(wide):
    return lax.rsqrt(jnp.mean(wide * wide, axis=-1, keepdims=True) + 1e-06)


def rms_scale(wide, gain):
    return wide * rms(wide) * gain


def picks(source, width):
    return jnp.asarray(np.asarray(source).reshape(-1, 1) == np.arange(width), BF16)


class Plan:
    def __init__(self, orbit, space, views, cols, chans, slice_chans):
        self.orbit, self.space, self.views = orbit, space, views
        self.cols, self.chans, self.slice_chans = cols, chans, slice_chans
        self.x = space // CORES
        share = cols // orbit
        self.by_column = share % CORES == 0
        self.ncol = share // CORES if self.by_column else share
        self.rows = space if self.by_column else self.x
        self.strided = self.by_column and self.ncol == 1 and slice_chans % 128 == 0
        self.pixels = self.rows * self.ncol
        self.pairs = views // 2
        self.down_rows = self.pairs * orbit * self.pixels
        self.send_rows = views * self.pixels
        self.peers = orbit * self.rows
        self.back = self.pairs * self.ncol
        self.lanes = next(n for n in (1, 2, 4, 8) if self.back * n % 8 == 0)
        self.back_rows, self.back_width = self.back * self.lanes, chans // self.lanes
        self.tiled = self.back_width % 128 == 0

    def column(self, o, core, c):
        return (o * CORES + core) * self.ncol + c if self.by_column else o * self.ncol + c

    def send_order(self):
        o, core, odd, r, pair, c = np.indices((self.orbit, CORES, 2, self.rows, self.pairs, self.ncol))
        row = r if self.by_column else r * CORES + core
        source = (row * self.views + 2 * pair + odd) * self.cols + self.column(o, core, c)
        return picks(source, self.space * self.views * self.cols)

    def end_order(self):
        o, s, lane, view, c = np.indices((self.orbit, self.rows, self.lanes, self.pairs, self.ncol))
        target = (lane * self.pairs + view) * self.cols + self.column(o, s % CORES, c)
        count = self.lanes * self.pairs * self.cols
        return jnp.asarray(target.reshape(1, -1) == np.arange(count).reshape(-1, 1), BF16)


def turn_conv_kernel(weight_ref, out_ref):
    taps, _, depth, chans = weight_ref.shape
    for i in range(taps):
        out_ref[i] = weight_ref[i].reshape(taps * depth, chans).T


def add_rows(plan, blocks, places, weight_ref, total):
    per_row, cols, depth = plan.views * plan.cols, plan.cols, plan.slice_chans
    rows = jnp.concatenate(blocks)
    count = rows.shape[0]
    column = lax.broadcasted_iota(jnp.int32, (count, 1), 0) & (cols - 1)
    for i in range(3):
        part = dot(rows, weight_ref[i])
        left, middle, right = [part[:, j * depth : (j + 1) * depth] for j in range(3)]
        left = jnp.where(column == 0, 0.0, pltpu.roll(left, 1, 0))
        right = jnp.where(column == cols - 1, 0.0, pltpu.roll(right, count - 1, 0))
        part = left + middle + right
        for n, place in enumerate(places):
            start = pl.multiple_of((place + 2 - i) * per_row, per_row)
            total[pl.ds(start, per_row)] += part[n * per_row : (n + 1) * per_row]


def early_kernel(plan, gain_ref, weight_ref, *refs):
    raw_refs, total_ref = refs[:-1], refs[-1]
    gain, space = gain_ref[...], lax.axis_index("space")
    blocks = [rms_scale(ref[...].astype(F32), gain).astype(BF16) for ref in raw_refs]
    places = [space, space ^ 1] + [space ^ (x * CORES) for x in range(1, plan.x)]
    total_ref[...] = jnp.zeros_like(total_ref)
    add_rows(plan, blocks, places, weight_ref, total_ref)


def late_kernel(plan, gain_ref, weight_ref, early_ref, *refs):
    order_refs, raw_refs, (out_ref, total, tiles) = refs[: 1 - plan.strided], refs[1 - plan.strided : -3], refs[-3:]
    gain, space = gain_ref[...], lax.axis_index("space")
    blocks = [rms_scale(ref[...].astype(F32), gain).astype(BF16) for ref in raw_refs]
    places = [space ^ (x * CORES + 1) for x in range(1, plan.x)]
    total[...] = early_ref[...]
    add_rows(plan, blocks, places, weight_ref, total)
    per_row, cols, depth = plan.views * plan.cols, plan.cols, plan.slice_chans
    if plan.strided:
        lanes = [slice(k * 128, (k + 1) * 128) for k in range(depth // 128)]
        for k, lane in enumerate(lanes):
            whole = total[per_row : (plan.space + 1) * per_row, lane]
            tiles[k] = whole / (1.0 + jnp.exp(-whole))
        half = plan.send_rows // 2
        for column in range(cols):
            for k, lane in enumerate(lanes):
                picked = [tiles[k, pl.ds(odd * cols + column, half, stride=2 * cols), :] for odd in range(2)]
                out_ref[column * plan.send_rows : (column + 1) * plan.send_rows, lane] = jnp.concatenate(picked).astype(BF16)
    else:
        whole = total[per_row : (plan.space + 1) * per_row]
        activated = (whole / (1.0 + jnp.exp(-whole))).astype(BF16)
        out_ref[...] = dot(order_refs[0][...], activated).astype(BF16)


def temporal_kernel(plan, got_ref, own_ref, other_ref, out_ref):
    core = lax.rem(lax.axis_index("space"), CORES)
    half, depth = plan.send_rows // 2, plan.slice_chans
    row = lax.broadcasted_iota(jnp.int32, (plan.down_rows, 1), 0)
    first = (row & (plan.back - 1)) < plan.ncol
    total = None
    for index, weight_ref in ((core, own_ref), (1 - core, other_ref)):
        block = got_ref[:, index].astype(F32)
        even = block[:, :half].reshape(plan.down_rows, depth)
        odd = block[:, half:].reshape(plan.down_rows, depth)
        before = jnp.where(first, pltpu.roll(odd, half - plan.back + plan.ncol, 0), pltpu.roll(odd, plan.ncol, 0))
        for k, rows in enumerate((before, even, odd)):
            part = dot(rows.astype(BF16), weight_ref[k])
            total = part if total is None else total + part
    out_ref[...] = total.astype(BF16)


def turn_kernel(own_ref, other_ref, out_ref):
    kinds, depth, chans = own_ref.shape
    for k, ref in enumerate((own_ref, other_ref)):
        out_ref[k] = ref[...].reshape(kinds * depth, chans).T


def attend_kernel(plan, gain_ref, qkv_ref, own_out, other_out, *refs):
    down_refs, (out_ref, tiles, leaving) = refs[:-3], refs[-3:]
    rows, depth = plan.down_rows, plan.slice_chans
    heads = depth // HD
    down = down_refs[0][...].astype(F32)
    for ref in down_refs[1:]:
        down = down + ref[...].astype(F32)
    down = down.astype(BF16).astype(F32)
    gained, scale = (down * gain_ref[...]).astype(BF16), rms(down)
    channel_head = lax.broadcasted_iota(jnp.int32, (1, depth), 1) >> (HD.bit_length() - 1)
    key_head = lax.broadcasted_iota(jnp.int32, (1, heads * rows), 1) >> (rows.bit_length() - 1)
    key_row_head = lax.broadcasted_iota(jnp.int32, (heads * rows, 1), 0) >> (rows.bit_length() - 1)
    spread = jnp.where(key_row_head == channel_head, 1.0, 0.0).astype(BF16)

    def by_head(block):
        wide = block.astype(F32)
        return jnp.concatenate([jnp.where(channel_head == h, wide, 0.0) for h in range(heads)]).astype(BF16)

    def pixel(number):
        return (number & (plan.ncol - 1)) + ((number >> (plan.back.bit_length() - 1)) & (plan.rows - 1)) * plan.ncol

    query_pixel = pixel(lax.broadcasted_iota(jnp.int32, (rows, 1), 0))
    key_pixel = pixel(lax.broadcasted_iota(jnp.int32, (1, heads * rows), 1) & (rows - 1))
    same = query_pixel == key_pixel
    first = lax.axis_index("space") < CORES
    projected = jnp.where(first, 1.0, 0.0) * down
    both = range(CORES)
    qkv = [(dot(gained, qkv_ref[k]) * scale).astype(BF16) for k in both]
    keys = [by_head(qkv[k][:, depth : 2 * depth]) for k in both]
    values = [by_head(qkv[k][:, 2 * depth :]) for k in both]
    scores = [dot_trans(qkv[k][:, :depth], keys[k]) * (HD**-0.5) for k in both]
    weights = []
    for score in scores:
        score = jnp.where(same, score, -jnp.inf)
        top = None
        for h in range(heads):
            peak = jnp.max(jnp.where(key_head == h, score, -jnp.inf), axis=-1, keepdims=True)
            top = peak if h == 0 else jnp.where(key_head >= h, peak, top)
        weights.append(jnp.exp(score - top).astype(BF16))
    mixed = [(dot(w, v) / dot(w, spread)).astype(BF16) for w, v in zip(weights, values)]
    projected = projected + dot(mixed[0], own_out[...]) + dot(mixed[1], other_out[...])
    width = plan.back_width
    if plan.tiled:
        for lane in range(plan.chans // 128):
            tiles[lane] = projected[:, lane * 128 : (lane + 1) * 128]
        wide = width // 128
        for lane in range(plan.chans // 128):
            for t in range(plan.back):
                source = tiles[lane, pl.ds(t, plan.peers, stride=plan.back), :]
                leaving[lane % wide, pl.ds(lane // wide * plan.back + t, plan.peers, stride=plan.back_rows), :] = source
        for lane in range(wide):
            out_ref[:, lane * 128 : (lane + 1) * 128] = leaving[lane].astype(BF16)
    else:
        parts = [projected[:, k * width : (k + 1) * width] for k in range(plan.lanes)]
        parts = [part.reshape(plan.peers, plan.back, width) for part in parts]
        out_ref[...] = jnp.concatenate(parts, axis=1).reshape(plan.peers * plan.back_rows, width).astype(BF16)


def end_kernel(plan, got_ref, order_ref, latents_ref, out_ref):
    rows = plan.pairs * plan.cols
    bottom = dot(order_ref[...], got_ref[...])
    bottom = jnp.concatenate([bottom[k * rows : (k + 1) * rows] for k in range(plan.lanes)], axis=1)
    bottom = bottom.astype(BF16).astype(F32)
    for f in range(plan.views):
        block = bottom[(f // 2) * plan.cols : (f // 2 + 1) * plan.cols]
        out_ref[f] = (latents_ref[f].astype(F32) + block).astype(BF16)


def call(kernel, name, shapes, args, scratch=(), flops=0, space=pltpu.VMEM):
    outs = [s if isinstance(s, jax.ShapeDtypeStruct) else jax.ShapeDtypeStruct(s, BF16) for s in shapes]
    moved = sum(a.size * a.dtype.itemsize for a in (*args, *outs))
    return pl.pallas_call(
        kernel,
        out_shape=outs,
        in_specs=[pl.BlockSpec(memory_space=space)] * len(args),
        out_specs=[pl.BlockSpec(memory_space=pltpu.VMEM)] * len(outs),
        scratch_shapes=list(scratch),
        compiler_params=pltpu.CompilerParams(vmem_limit_bytes=16 * 2**20),
        cost_estimate=pl.CostEstimate(flops=flops, bytes_accessed=moved, transcendentals=0),
        name=name,
    )(*args)


def body(latents, conv_gain, spatial_weight, temporal_weight, attn_gain, qkv_weight, out_weight):
    views, _, cols, chans = latents.shape
    orbit, space = lax.axis_size("orbit"), lax.axis_size("space")
    plan = Plan(orbit, space, views, cols, chans, spatial_weight.shape[2])
    conv_gain, attn_gain = conv_gain.reshape(1, chans), attn_gain.reshape(1, chans)

    def swap(block, distance):
        return lax.ppermute(block, "space", [(s, s ^ distance) for s in range(space)])

    def exchange(blocks, groups):
        return lax.all_to_all(blocks, ("orbit", "space"), 0, 0, tiled=True, axis_index_groups=groups)

    by_core = [[o * space + x * CORES + c for o in range(orbit) for c in range(CORES)] for x in range(plan.x)]
    by_x = [[o * space + x * CORES + c for o in range(orbit) for x in range(plan.x)] for c in range(CORES)]

    own = latents.reshape(views * cols, chans)
    far = [swap(own, x * CORES) for x in range(1, plan.x)]
    near = swap(own, 1)
    depth, per_row = plan.slice_chans, views * cols
    (taps,) = call(turn_conv_kernel, "turn_conv", [(3, chans, 3 * depth)], (spatial_weight,), flops=60 * 10**9)
    other_temporal, other_out = swap(temporal_weight, 1), swap(out_weight, 1)
    far, near, taps = lax.optimization_barrier((far, near, taps))
    across = [swap(block, 1) for block in far]
    total_shape = ((space + 2) * per_row, depth)
    order = [] if plan.strided else [plan.send_order()]
    (early,) = call(
        functools.partial(early_kernel, plan),
        "conv_early",
        [jax.ShapeDtypeStruct(total_shape, F32)],
        (conv_gain, taps, own, near, *far),
        flops=6 * 10**9,
    )
    count = space * per_row
    (activated,) = call(
        functools.partial(late_kernel, plan),
        "conv_late",
        [(count, depth)],
        (conv_gain, taps, early, *order, *across),
        [pltpu.VMEM(total_shape, F32), pltpu.VMEM((max(depth // 128, 1), count, 128), F32)],
        flops=2 * 9 * count * chans * depth,
    )
    swapped = (other_temporal, other_out)
    activated, swapped, qkv = lax.optimization_barrier((activated, swapped, qkv_weight))
    (other_temporal, other_out), other_qkv = swapped, swap(qkv, 1)
    got = exchange(activated.reshape(orbit * CORES, plan.send_rows, plan.slice_chans), by_core)
    (down,) = call(
        functools.partial(temporal_kernel, plan),
        "temporal",
        [(plan.down_rows, chans)],
        (got.reshape(orbit, CORES, plan.send_rows, plan.slice_chans), temporal_weight, other_temporal),
        flops=2 * 6 * plan.down_rows * chans * plan.slice_chans,
    )
    down, own_qkv, other_qkv = lax.optimization_barrier((down, qkv_weight, other_qkv))
    downs = [down] + [swap(down, x * CORES) for x in range(1, plan.x)]
    (qkv,) = call(
        turn_kernel,
        "turn",
        [(2, chans, 3 * plan.slice_chans)],
        (own_qkv, other_qkv),
        flops=6 * 10**9,
    )
    peers = plan.peers
    (back,) = call(
        functools.partial(attend_kernel, plan),
        "attend",
        [(peers * plan.back_rows, plan.back_width)],
        (attn_gain, qkv, out_weight, other_out, *downs),
        [
            pltpu.VMEM((chans // 128, plan.down_rows, 128), F32),
            pltpu.VMEM((max(plan.back_width // 128, 1), peers * plan.back_rows, 128), F32),
        ],
        flops=2 * 8 * plan.down_rows * chans * plan.slice_chans,
    )
    got = exchange(back.reshape(peers, plan.back_rows, plan.back_width), None if plan.by_column else by_x)
    (restored,) = call(
        functools.partial(end_kernel, plan),
        "restore",
        [(views, cols, chans)],
        (got.reshape(peers * plan.back_rows, plan.back_width), plan.end_order(), latents.reshape(views, cols, chans)),
    )
    return restored.reshape(latents.shape)


def solution(mesh):
    return jax.shard_map(
        body,
        mesh=mesh,
        in_specs=(
            P("orbit", "space", None, None),
            P(),
            P(None, None, "space", None),
            P(None, "space", None),
            P(),
            P(None, "space", None),
            P("space", None),
        ),
        out_specs=P("orbit", "space", None, None),
        check_vma=False,
    )
```
